256 devices in a mesh: pb: 64 (over y, z, x_lo), ka: 4 (over x_hi, core).
Axes of the slice: x: 4 (x_hi: 2, x_lo: 2; x = x_hi * 2 + x_lo), y: 4, z: 8, core: 2. Of those that a mesh axis runs over, the one named last changes fastest.
Arguments:
- queries: bfloat16 [16384, 4096], P('pb', 'ka'), may hold values from -25 to 25
- output_gradient: bfloat16 [16384, 4096], P('pb', 'ka'), may hold values from -6 to 6
- key_states: bfloat16 [16384, 2048], P(('pb', 'ka')), may hold values from -6 to 6
- value_inputs: bfloat16 [16384, 2048], P(('pb', 'ka')), may hold values from -6 to 6
- turn_ids: int32 [16384], replicated, may hold values from 0 to 31, never falling along the last dimension, each value on 1 to 1792 neighbouring positions
- listed: int32 [2, 128, 14], replicated, may hold values 0 or 1
Outputs:
- grad_queries: float32 [16384, 4096], P('pb', 'ka')
- grad_keys: float32 [16384, 2048], P(('pb', 'ka'))
- grad_values: float32 [16384, 2048], P(('pb', 'ka'))
The draws below stay inside these ranges and needn't reach their ends.
Inputs may be any that keep to these rules, and one draw needn't show every extreme that they name: `turn_ids`: turn numbers never fall along the window; every turn spans 1 to 1792 positions, and some turn spans exactly 1792.
All inputs are finite; a program needn't handle non-finite values.
Results may differ from the reference program's by a relative error of at most 0.003.
Values may be sent and summed in bfloat16 or wider, within the bound.
No kernel may reach another device: no remote copies, remote signals or barrier semaphores. Data moves between devices by JAX's collectives and lax.ppermute only.
A program may use at most 128 MiB of HBM per device.

```python
import math
import jax
import jax.numpy as jnp
import numpy as np
from jax import lax

QUERY_HEADS = 32
KEY_VALUE_HEADS = 16
HEAD_SIZE = 128
HEAD_GROUPS = 2
BLOCK_POSITIONS = 128
BACK = 14
WINDOW_TOKENS = 16384
NB = 128


def shared_rows(key):
    pick_key, sign_key, power_key = jax.random.split(key, 3)
    chosen = jax.random.bernoulli(pick_key, 1.0 / 64.0, (WINDOW_TOKENS,))
    sign_rows = jnp.where(jax.random.bernoulli(sign_key, 0.5, (WINDOW_TOKENS, HEAD_SIZE)), 1.0, -1.0)
    strength = jax.random.uniform(power_key, (WINDOW_TOKENS,), minval=6.5, maxval=25.0)
    return (chosen, sign_rows, strength)


def draw_queries(key, part):
    self_key = jax.random.fold_in(key, 11)
    regular_portion = jnp.clip(jax.random.normal(self_key, (WINDOW_TOKENS, QUERY_HEADS * HEAD_SIZE), jnp.float32), -5.0, 5.0)
    chosen, sign_rows, strength = shared_rows(key)
    aligned = jnp.tile(strength[:, None] * sign_rows, (1, QUERY_HEADS))
    scaled = regular_portion
    drawn = jnp.where(chosen[:, None], aligned, scaled)
    return drawn.astype(jnp.bfloat16)


def draw_key_states(key, part):
    self_key = jax.random.fold_in(key, 23)
    regular_portion = jnp.clip(jax.random.normal(self_key, (WINDOW_TOKENS, KEY_VALUE_HEADS * HEAD_SIZE), jnp.float32), -5.0, 5.0)
    chosen, sign_rows, strength = shared_rows(key)
    magnitude = min(6.0, 192.0 / HEAD_SIZE)
    next_chosen = jnp.roll(chosen, -1)
    next_signs = jnp.roll(sign_rows, -1, axis=0)
    next_strength = jnp.roll(strength, -1)
    near_rows = magnitude * next_signs * (1.0 - 0.125 / next_strength)[:, None]
    exact_rows = magnitude * sign_rows
    value_per_head = jnp.where(chosen[:, None], exact_rows, near_rows)
    repeated_rows = jnp.tile(value_per_head, (1, KEY_VALUE_HEADS))
    scaled = regular_portion
    drawn = jnp.where((chosen | next_chosen)[:, None], repeated_rows, scaled)
    return drawn.astype(jnp.bfloat16)


def with_ends(values, own_key, smallest, high):
    longest = values.shape.index(max(values.shape))
    spots = []
    for shift in (0, 1):
        where = [jax.random.randint(jax.random.fold_in(own_key, axis), (), 0, length) for axis, length in enumerate(values.shape)]
        where[longest] = (where[longest] + shift) % values.shape[longest]
        spots.append(tuple(where))
    return values.at[spots[0]].set(smallest).at[spots[1]].set(high)


def block_levels(rng, extent, cuts, smallest, largest):
    loudness = 1.0
    for dim, parts in cuts:
        draws = jax.random.uniform(jax.random.fold_in(jax.random.fold_in(rng, 6), dim), (parts,), jnp.float32, smallest / len(cuts), largest / len(cuts))
        loudness = loudness * jnp.repeat(jnp.exp(draws), extent[dim] // parts).reshape((-1,) + (1,) * (len(extent) - 1 - dim))
    return loudness


def split_up(count, total, limit, lean):
    portions = [(1 << 20) // math.isqrt(grade ** lean) + 1 for grade in range(2, count + 1)]
    rest, holding = total - limit - (count - 1), [1] * (count - 1)
    while rest > 0:
        free = [i for i in range(count - 1) if holding[i] < limit]
        mass, budget = sum([portions[i] for i in free]), rest
        for i in free:
            more = min(limit - holding[i], max(1, budget * portions[i] // mass), rest)
            holding[i] = holding[i] + more
            rest = rest - more
    return np.array([limit] + holding)


def ragged(own_key, number_of, total, reach, lean):
    if number_of == 2:
        one = jax.random.randint(own_key, (), max(1, total - reach), min(reach, total - 1) + 1)
        return jnp.stack([one, total - one])
    lengths = jnp.asarray(split_up(number_of, total, reach, lean), jnp.int32)
    pairs = (number_of - 1) // 2
    donor, receiver = lengths[1:1 + 2 * pairs:2], lengths[2:2 + 2 * pairs:2]
    room = jnp.minimum(donor - 1, reach - receiver)
    passed = jax.random.randint(jax.random.fold_in(own_key, 1), (pairs,), 0, 1 << 20) % (room + 1)
    lengths = lengths.at[1:1 + 2 * pairs:2].set(donor - passed).at[2:2 + 2 * pairs:2].set(receiver + passed)
    return lengths[jax.random.permutation(jax.random.fold_in(own_key, 2), number_of)]


def gaussian(own_key, extent, spread, limit, cuts=(), kind=jnp.bfloat16):
    values = spread * jax.random.normal(own_key, extent, jnp.float32)
    if cuts:
        values = values * block_levels(own_key, extent, cuts, -0.22, 0.18)
    return jnp.clip(values, -limit, limit).astype(kind)


def setup_inputs(seed: int = 0) -> dict:
    streams_of = jax.random.split(jax.random.key(seed), 7)
    return {
        "queries": draw_queries(jax.random.fold_in(streams_of[6], 71), 0),
        "output_gradient": gaussian(streams_of[1], (WINDOW_TOKENS, QUERY_HEADS * HEAD_SIZE), 1.0, 6.0, ((0, 64), (1, 4))),
        "key_states": draw_key_states(jax.random.fold_in(streams_of[6], 71), 0),
        "value_inputs": gaussian(streams_of[3], (WINDOW_TOKENS, KEY_VALUE_HEADS * HEAD_SIZE), 1.0, 6.0, ((0, 256),)),
        "turn_ids": jnp.searchsorted(jnp.cumsum(ragged(streams_of[4], WINDOW_TOKENS // (4 * BLOCK_POSITIONS), WINDOW_TOKENS, BACK * BLOCK_POSITIONS, 2)), jnp.arange(WINDOW_TOKENS), side="right").astype(jnp.int32),
        "listed": with_ends((jax.random.randint(streams_of[5], (HEAD_GROUPS, NB, BACK), 0, 2) < 1).astype(jnp.int32), jax.random.fold_in(streams_of[5], 1), 0, 1),
    }


SCORE_SCALE = 1.0 / 12.0
NEG_LARGE = -1.0e30


def visible_mask(turn_ids, listed, query_begin, key_pos, tok_rows):
    query_pos = query_begin + jnp.arange(tok_rows, dtype=jnp.int32)
    query_turn = lax.dynamic_slice_in_dim(turn_ids, query_begin, tok_rows, 0)
    key_turn = turn_ids[jnp.clip(key_pos, 0, turn_ids.shape[0] - 1)]
    blk_count = tok_rows // BLOCK_POSITIONS
    query_blocks = query_begin // BLOCK_POSITIONS + jnp.arange(blk_count, dtype=jnp.int32)
    list_table = lax.dynamic_slice_in_dim(listed, query_begin // BLOCK_POSITIONS, blk_count, 1)
    offsets = query_blocks[:, None] - key_pos[None, :] // BLOCK_POSITIONS - 1
    onehot = (offsets[:, :, None] == jnp.arange(BACK, dtype=jnp.int32)[None, None, :]).astype(jnp.float32)
    listed_hit = jnp.einsum("gbo,bko->gbk", list_table.astype(jnp.float32), onehot) > 0.5
    listed_hit = jnp.repeat(listed_hit, BLOCK_POSITIONS, axis=1)
    causal_ok = (key_pos[None, :] <= query_pos[:, None]) & (key_pos[None, :] >= 0)
    same_turn = query_turn[:, None] == key_turn[None, :]
    return causal_ok[None] & (same_turn[None] | listed_hit)


def reference(queries, output_gradient, key_states, value_inputs, turn_ids, listed):
    group_width = QUERY_HEADS // KEY_VALUE_HEADS
    group_head_count = KEY_VALUE_HEADS // HEAD_GROUPS
    padding_rows = BACK * BLOCK_POSITIONS
    key_extent = (BACK + 1) * BLOCK_POSITIONS
    empty_rows = jnp.zeros((padding_rows, KEY_VALUE_HEADS * HEAD_SIZE), jnp.bfloat16)
    key_padded_rows = jnp.concatenate([empty_rows, key_states], axis=0)
    value_padded_rows = jnp.concatenate([empty_rows, value_inputs], axis=0)

    def per_block(running, blk_index):
        key_gradient, value_gradient = running
        query_begin = blk_index * BLOCK_POSITIONS
        query_block = lax.dynamic_slice_in_dim(queries, query_begin, BLOCK_POSITIONS, 0).astype(jnp.float32).reshape(BLOCK_POSITIONS, KEY_VALUE_HEADS, group_width, HEAD_SIZE)
        block_gradient = lax.dynamic_slice_in_dim(output_gradient, query_begin, BLOCK_POSITIONS, 0).astype(jnp.float32).reshape(BLOCK_POSITIONS, KEY_VALUE_HEADS, group_width, HEAD_SIZE)
        window_keys = lax.dynamic_slice_in_dim(key_padded_rows, query_begin, key_extent, 0).astype(jnp.float32).reshape(key_extent, KEY_VALUE_HEADS, HEAD_SIZE)
        window_values = lax.dynamic_slice_in_dim(value_padded_rows, query_begin, key_extent, 0).astype(jnp.float32).reshape(key_extent, KEY_VALUE_HEADS, HEAD_SIZE)
        key_pos = query_begin - padding_rows + jnp.arange(key_extent, dtype=jnp.int32)
        allowed = visible_mask(turn_ids, listed, query_begin, key_pos, BLOCK_POSITIONS)
        allowed_heads = jnp.repeat(allowed, group_head_count, axis=0)[:, None]
        raw_scores = jnp.einsum("rhqd,khd->hqrk", query_block, window_keys) * SCORE_SCALE
        scores = jnp.where(allowed_heads, raw_scores, NEG_LARGE)
        peak_max = jnp.max(scores, axis=3, keepdims=True)
        weights = jnp.where(allowed_heads, jnp.exp(scores - peak_max), 0.0)
        soft_prob = weights / jnp.sum(weights, axis=3, keepdims=True)
        grad_prob = jnp.einsum("rhqd,khd->hqrk", block_gradient, window_values)
        delta_row = jnp.sum(soft_prob * grad_prob, axis=3, keepdims=True)
        blended_rows = (SCORE_SCALE * soft_prob * (grad_prob - delta_row)).astype(jnp.bfloat16)
        blended_rows = lax.optimization_barrier(blended_rows).astype(jnp.float32)
        probability_floor = lax.optimization_barrier(soft_prob.astype(jnp.bfloat16)).astype(jnp.float32)
        grad_q_blk = jnp.einsum("hqrk,khd->rhqd", blended_rows, window_keys).reshape(BLOCK_POSITIONS, QUERY_HEADS * HEAD_SIZE)
        window_key_gradient = jnp.einsum("tmev,etmi->vti", blended_rows, query_block).reshape(key_extent, KEY_VALUE_HEADS * HEAD_SIZE)
        window_value_gradient = jnp.einsum("tmev,etmi->vti", probability_floor, block_gradient).reshape(key_extent, KEY_VALUE_HEADS * HEAD_SIZE)
        key_gradient = lax.dynamic_update_slice_in_dim(key_gradient, lax.dynamic_slice_in_dim(key_gradient, query_begin, key_extent, 0) + window_key_gradient, query_begin, 0)
        value_gradient = lax.dynamic_update_slice_in_dim(value_gradient, lax.dynamic_slice_in_dim(value_gradient, query_begin, key_extent, 0) + window_value_gradient, query_begin, 0)
        return (key_gradient, value_gradient), grad_q_blk

    initial_state = (jnp.zeros((WINDOW_TOKENS + padding_rows, KEY_VALUE_HEADS * HEAD_SIZE), jnp.float32), jnp.zeros((WINDOW_TOKENS + padding_rows, KEY_VALUE_HEADS * HEAD_SIZE), jnp.float32))
    (key_gradient, value_gradient), grad_q_blocks = lax.scan(per_block, initial_state, jnp.arange(NB, dtype=jnp.int32))
    return grad_q_blocks.reshape(WINDOW_TOKENS, QUERY_HEADS * HEAD_SIZE), key_gradient[padding_rows:], value_gradient[padding_rows:]
```

```python
import functools
import math

import jax
import jax.numpy as jnp
from jax import lax
from jax.experimental import pallas as pl
from jax.experimental.pallas import tpu as pltpu
from jax.sharding import Mesh
from jax.sharding import PartitionSpec as P

QUERY_HEADS = 32
KEY_VALUE_HEADS = 16
HEAD_SIZE = 128
HEAD_GROUPS = 2
BLOCK = 128
BACK = 14
SPAN = 256
SLAB = 2 * SPAN
HALO = BACK * BLOCK
WINDOW = HALO + SLAB
LOCAL_HEADS = 2
Q_BLOCKS = SLAB // BLOCK
K_BLOCKS = BACK + 1

SCORE_SCALE = 1.0 / 12.0
EXP2_SCALE = SCORE_SCALE * math.log2(math.e)
NEG_LARGE = -1e30

SLAB_AXES = ("y", "z")
MEMBER_AXES = ("xl", "xh", "core")


def slab_shift(x, by):
    count = lax.axis_size(SLAB_AXES)
    return lax.ppermute(x, SLAB_AXES, [(i, (i + by) % count) for i in range(count)])


def dot(a, b, contract):
    return lax.dot_general(a, b, ((contract[0], contract[1]), ((), ())), preferred_element_type=jnp.float32)


def attention_kernel(
    hit_ref, start_ref, q_ref, do_ref, p4_ref, p3_ref, p2_ref, p1_ref, p0_ref, dq_ref, dkv_ref,
    win, s_scr, dp_scr, ds_scr, p_scr,
):
    row = 0
    for piece in (p4_ref, p3_ref, p2_ref, p1_ref, p0_ref):
        rows = piece.shape[0]
        win[row : row + rows, :] = piece[...]
        row += rows
    dkv_ref[...] = jnp.zeros_like(dkv_ref)
    key_iota = lax.broadcasted_iota(jnp.int32, (BLOCK, BLOCK), 0)
    row_iota = lax.broadcasted_iota(jnp.int32, (BLOCK, BLOCK), 1)

    def step(t, carry):
        h = t // Q_BLOCKS
        i = t % Q_BLOCKS
        row0 = pl.multiple_of(i * BLOCK, BLOCK)
        lane0 = pl.multiple_of(h * HEAD_SIZE, HEAD_SIZE)
        vlane0 = pl.multiple_of((h + LOCAL_HEADS) * HEAD_SIZE, HEAD_SIZE)
        qlane0 = pl.multiple_of(h * 2 * HEAD_SIZE, HEAD_SIZE)
        qlane1 = pl.multiple_of(h * 2 * HEAD_SIZE + HEAD_SIZE, HEAD_SIZE)

        def both(ref):
            return jnp.concatenate(
                [
                    ref[pl.ds(row0, BLOCK), pl.ds(qlane0, HEAD_SIZE)],
                    ref[pl.ds(row0, BLOCK), pl.ds(qlane1, HEAD_SIZE)],
                ],
                axis=0,
            )

        qs = both(q_ref)
        dos = both(do_ref)
        start = start_ref[0:1, pl.ds(row0, BLOCK)] - row0

        def keys(w):
            return win[pl.ds(pl.multiple_of(row0 + w * BLOCK, BLOCK), BLOCK), pl.ds(lane0, HEAD_SIZE)]

        def values(w):
            return win[pl.ds(pl.multiple_of(row0 + w * BLOCK, BLOCK), BLOCK), pl.ds(vlane0, HEAD_SIZE)]

        peak = jnp.full((8, 2 * BLOCK), NEG_LARGE, jnp.float32)
        for w in range(K_BLOCKS):
            s = dot(keys(w), qs, ((1,), (1,)))
            if w < BACK:
                bound = jnp.where(hit_ref[i, w] > 0, -1, start - w * BLOCK)
                ok = key_iota >= bound
            else:
                ok = (key_iota >= start - w * BLOCK) & (key_iota <= row_iota)
            ok = jnp.concatenate([ok, ok], axis=1)
            s = jnp.where(ok, s * EXP2_SCALE, NEG_LARGE)
            s_scr[w * BLOCK : (w + 1) * BLOCK, :] = s
            peak = jnp.maximum(peak, jnp.max(s.reshape(BLOCK // 8, 8, 2 * BLOCK), axis=0))
        peak = jnp.max(peak, axis=0, keepdims=True)

        total = jnp.zeros((8, 2 * BLOCK), jnp.float32)
        inner = jnp.zeros((8, 2 * BLOCK), jnp.float32)
        for w in range(K_BLOCKS):
            rows = slice(w * BLOCK, (w + 1) * BLOCK)
            dp = dot(values(w), dos, ((1,), (1,)))
            weight = jnp.exp2(s_scr[rows, :] - peak)
            total += jnp.sum(weight.reshape(BLOCK // 8, 8, 2 * BLOCK), axis=0)
            inner += jnp.sum((weight * dp).reshape(BLOCK // 8, 8, 2 * BLOCK), axis=0)
            s_scr[rows, :] = weight
            dp_scr[rows, :] = dp
        total = jnp.sum(total, axis=0, keepdims=True)
        inner = jnp.sum(inner, axis=0, keepdims=True)
        inverse = 1.0 / total
        delta = inner * inverse
        inverse_scaled = inverse * SCORE_SCALE

        for w in range(K_BLOCKS):
            rows = slice(w * BLOCK, (w + 1) * BLOCK)
            weight = s_scr[rows, :]
            p_scr[rows, :] = (weight * inverse).astype(jnp.bfloat16)
            ds_scr[rows, :] = ((weight * inverse_scaled) * (dp_scr[rows, :] - delta)).astype(jnp.bfloat16)
        dq_t = jnp.zeros((HEAD_SIZE, 2 * BLOCK), jnp.float32)
        for w in range(K_BLOCKS):
            rows = slice(w * BLOCK, (w + 1) * BLOCK)
            out_rows = pl.ds(pl.multiple_of(row0 + w * BLOCK, BLOCK), BLOCK)
            ds = ds_scr[rows, :]
            dkv_ref[out_rows, pl.ds(lane0, HEAD_SIZE)] += dot(ds, qs, ((1,), (0,)))
            dkv_ref[out_rows, pl.ds(vlane0, HEAD_SIZE)] += dot(p_scr[rows, :], dos, ((1,), (0,)))
        window_keys = win[pl.ds(row0, K_BLOCKS * BLOCK), pl.ds(lane0, HEAD_SIZE)]
        dq_t = dot(window_keys, ds_scr[...], ((0,), (0,)))
        dq = dq_t.T
        dq_ref[pl.ds(row0, BLOCK), pl.ds(qlane0, HEAD_SIZE)] = dq[:BLOCK]
        dq_ref[pl.ds(row0, BLOCK), pl.ds(qlane1, HEAD_SIZE)] = dq[BLOCK:]
        return carry

    lax.fori_loop(0, LOCAL_HEADS * Q_BLOCKS, step, 0)


def attention(hit, start, q, do, pieces):
    vmem = pl.BlockSpec(memory_space=pltpu.VMEM)
    smem = pl.BlockSpec(memory_space=pltpu.SMEM)
    keys = K_BLOCKS * BLOCK
    return pl.pallas_call(
        attention_kernel,
        out_shape=(
            jax.ShapeDtypeStruct((SLAB, 4 * HEAD_SIZE), jnp.float32),
            jax.ShapeDtypeStruct((WINDOW, 4 * HEAD_SIZE), jnp.float32),
        ),
        in_specs=[smem] + [vmem] * 8,
        out_specs=(vmem, vmem),
        scratch_shapes=[
            pltpu.VMEM((WINDOW, 4 * HEAD_SIZE), jnp.bfloat16),
            pltpu.VMEM((keys, 2 * BLOCK), jnp.float32),
            pltpu.VMEM((keys, 2 * BLOCK), jnp.float32),
            pltpu.VMEM((keys, 2 * BLOCK), jnp.bfloat16),
            pltpu.VMEM((keys, 2 * BLOCK), jnp.bfloat16),
        ],
        compiler_params=pltpu.CompilerParams(vmem_limit_bytes=48 * 1024 * 1024),
        name="attention",
    )(hit, start, q, do, *pieces)


def per_device(queries, output_gradient, key_states, value_inputs, turn_ids, listed):
    slab = lax.axis_index(SLAB_AXES)
    low = lax.axis_index("xl")
    group = lax.axis_index("xh")
    width = LOCAL_HEADS * HEAD_SIZE

    def by_owner(x):
        return x.reshape(-1, 4, 2, width).transpose(2, 1, 0, 3)

    kv = jnp.concatenate([by_owner(key_states), by_owner(value_inputs)], axis=3)
    kv = kv.reshape(8, key_states.shape[0], 2 * width)
    own = lax.all_to_all(kv, MEMBER_AXES, 0, 0, tiled=True).reshape(SLAB, 2 * width)

    q2 = jnp.stack([queries, output_gradient]).reshape(2, SPAN, 2, 2 * width)
    mine = lax.dynamic_index_in_dim(q2, low, 2, keepdims=False)
    other = lax.dynamic_index_in_dim(q2, 1 - low, 2, keepdims=False)
    other = lax.ppermute(other, "xl", [(0, 1), (1, 0)])
    first = low == 0
    q_do = jnp.concatenate([jnp.where(first, mine, other), jnp.where(first, other, mine)], axis=1)

    p1 = slab_shift(own, 1)
    p2 = slab_shift(p1, 1)
    p3 = slab_shift(p2, 1)
    p4 = slab_shift(p3[SPAN:], 1)

    padded = jnp.concatenate([jnp.full((HALO,), -1, turn_ids.dtype), turn_ids])
    window_turns = lax.dynamic_slice_in_dim(padded, slab * SLAB, WINDOW, 0)
    start = jnp.sum((window_turns[None, :] < window_turns[HALO:, None]).astype(jnp.int32), axis=1)[None, :]
    table = lax.dynamic_index_in_dim(listed, group, 0, keepdims=False)
    table = lax.dynamic_slice_in_dim(table, slab * Q_BLOCKS, Q_BLOCKS, 0)[:, ::-1]
    key_block = slab * Q_BLOCKS - BACK + jnp.arange(Q_BLOCKS)[:, None] + jnp.arange(BACK)[None, :]
    hit = jnp.where(key_block >= 0, table, 0)

    dq, dkv = attention(hit, start, q_do[0], q_do[1], (p4, p3, p2, p1, own))

    part = [dkv[:SPAN]] + [dkv[SPAN + SLAB * k : SPAN + SLAB * (k + 1)] for k in range(4)]
    moving = slab_shift(part[0].astype(jnp.bfloat16), -1).astype(jnp.float32)
    moving = jnp.concatenate([part[1][:SPAN], part[1][SPAN:] + moving], axis=0)
    for k in (2, 3, 4):
        moving = part[k] + slab_shift(moving.astype(jnp.bfloat16), -1).astype(jnp.float32)

    out = lax.all_to_all(moving.reshape(8, -1, 2 * width), MEMBER_AXES, 0, 0, tiled=True)
    out = out.reshape(2, 4, -1, 2, width).transpose(3, 2, 1, 0, 4).reshape(2, -1, KEY_VALUE_HEADS * HEAD_SIZE)

    dq = dq.reshape(2, SPAN, 2 * width)
    mine = lax.dynamic_index_in_dim(dq, low, 0, keepdims=False)
    other = lax.dynamic_index_in_dim(dq, 1 - low, 0, keepdims=False)
    other = lax.ppermute(other, "xl", [(0, 1), (1, 0)])
    grad_queries = jnp.concatenate([jnp.where(first, mine, other), jnp.where(first, other, mine)], axis=1)
    return grad_queries, out[0], out[1]


def solution(mesh):
    y, z, xl, xh, core = 4, 8, 2, 2, 2
    fine = Mesh(mesh.devices.reshape(y, z, xl, xh, core), ("y", "z", "xl", "xh", "core"))
    pb, ka = ("y", "z", "xl"), ("xh", "core")
    in_specs = (P(pb, ka), P(pb, ka), P(pb + ka, None), P(pb + ka, None), P(), P())
    out_specs = (P(pb, ka), P(pb + ka, None), P(pb + ka, None))
    return jax.shard_map(per_device, mesh=fine, in_specs=in_specs, out_specs=out_specs, check_vma=False)
```

```python
import functools
import math

import jax
import jax.numpy as jnp
from jax import lax
from jax.experimental import pallas as pl
from jax.experimental.pallas import tpu as pltpu
from jax.sharding import Mesh
from jax.sharding import PartitionSpec as P

KEY_VALUE_HEADS = 16
HEAD_SIZE = 128
BLOCK = 128
BACK = 14
SPAN = 256
SLAB = 2 * SPAN
HALO = BACK * BLOCK
WINDOW = HALO + SLAB
LOCAL_HEADS = 2
WIDTH = LOCAL_HEADS * HEAD_SIZE
Q_BLOCKS = SLAB // BLOCK
PAIR = 2 * BLOCK
ROWS = Q_BLOCKS * PAIR

SCORE_SCALE = 1.0 / 12.0
EXP2_SCALE = SCORE_SCALE * math.log2(math.e)
NEG_LARGE = -1e30

SLAB_AXES = ("y", "z")
MEMBER_AXES = ("xl", "xh", "core")

VMEM_SPEC = pl.BlockSpec(memory_space=pltpu.VMEM)
SMEM_SPEC = pl.BlockSpec(memory_space=pltpu.SMEM)


def slab_shift(x, by):
    count = lax.axis_size(SLAB_AXES)
    return lax.ppermute(x, SLAB_AXES, [(i, i + by) for i in range(count) if 0 <= i + by < count])


def low_swap(x):
    return lax.ppermute(x, "xl", [(0, 1), (1, 0)])


def dot(a, b, da, db):
    return lax.dot_general(a, b, (((da,), (db,)), ((), ())), preferred_element_type=jnp.float32)


def call(kernel, name, out_shape, in_specs, scratch=(), aliases=None):
    outs = out_shape if isinstance(out_shape, (tuple, list)) else (out_shape,)
    size = sum(o.size * o.dtype.itemsize for o in outs)
    return pl.pallas_call(
        kernel,
        out_shape=out_shape,
        in_specs=in_specs,
        out_specs=jax.tree.map(lambda _: VMEM_SPEC, out_shape),
        scratch_shapes=scratch,
        input_output_aliases=aliases or {},
        compiler_params=pltpu.CompilerParams(vmem_limit_bytes=32 * 1024 * 1024),
        cost_estimate=pl.CostEstimate(flops=1024, bytes_accessed=size, transcendentals=0),
        name=name,
    )


def f32(*shape):
    return jax.ShapeDtypeStruct(shape, jnp.float32)


def bf16(*shape):
    return jax.ShapeDtypeStruct(shape, jnp.bfloat16)


def owner_columns(d):
    return (d % 4 * 4 + d // 4 * 2) * HEAD_SIZE


def pack_kernel(k_ref, v_ref, out_ref, k_scr, v_scr, sems):
    copies = [pltpu.make_async_copy(k_ref, k_scr, sems.at[0]), pltpu.make_async_copy(v_ref, v_scr, sems.at[1])]
    for copy in copies:
        copy.start()
    for n, (copy, scr) in enumerate(zip(copies, (k_scr, v_scr))):
        copy.wait()
        for d in range(8):
            c = owner_columns(d)
            out_ref[d, :, n * WIDTH : (n + 1) * WIDTH] = scr[:, c : c + WIDTH]


def unpack_kernel(in_ref, dk_ref, dv_ref):
    for d in range(8):
        c = owner_columns(d)
        dk_ref[:, c : c + WIDTH] = in_ref[d, :, :WIDTH].astype(jnp.float32)
        dv_ref[:, c : c + WIDTH] = in_ref[d, :, WIDTH:].astype(jnp.float32)


def rows_kernel(low_ref, q_ref, do_ref, other_ref, qr_ref, dor_ref):
    low = low_ref[0]
    for x, (src, dst) in enumerate(((q_ref, qr_ref), (do_ref, dor_ref))):
        for h in range(LOCAL_HEADS):
            for b in range(2):
                for n in range(2):
                    c = h * PAIR + n * BLOCK
                    rows = slice(b * BLOCK, (b + 1) * BLOCK)
                    here = pl.multiple_of((2 * low + b) * PAIR + n * BLOCK, BLOCK)
                    there = pl.multiple_of((2 * (1 - low) + b) * PAIR + n * BLOCK, BLOCK)
                    lane = pl.multiple_of(low * 2 * WIDTH + c, BLOCK)
                    dst[h, pl.ds(here, BLOCK), :] = src[rows, pl.ds(lane, BLOCK)]
                    dst[h, pl.ds(there, BLOCK), :] = other_ref[x, rows, c : c + BLOCK]


def columns_kernel(low_ref, mine_ref, other_ref, out_ref):
    low = low_ref[0]
    out_ref[:, pl.ds(pl.multiple_of(low * 2 * WIDTH, BLOCK), 2 * WIDTH)] = mine_ref[...]
    out_ref[:, pl.ds(pl.multiple_of((1 - low) * 2 * WIDTH, BLOCK), 2 * WIDTH)] = other_ref[...]


def visible(i, w):
    return i <= w <= i + BACK


def mask_of(hit_ref, start_ref, i, w):
    key_iota = lax.broadcasted_iota(jnp.int32, (BLOCK, BLOCK), 0)
    bound = start_ref[0:1, i * BLOCK : (i + 1) * BLOCK] - w * BLOCK
    if w < i + BACK:
        ok = key_iota >= jnp.where(hit_ref[i, w - i] > 0, -1, bound)
    else:
        ok = (key_iota >= bound) & (key_iota <= lax.broadcasted_iota(jnp.int32, (BLOCK, BLOCK), 1))
    return jnp.concatenate([ok, ok], axis=1)


def fold(x, op):
    return op(x.reshape(BLOCK // 8, 8, PAIR), axis=0)


def stats_kernel(first_blocks, opening, closing, *refs):
    count = len(first_blocks)
    hit_ref, start_ref, q_ref, do_ref = refs[:4]
    pieces = refs[4 : 4 + count]
    rest = refs[4 + count :]
    if opening:
        state_in, rest = None, rest
    else:
        state_in, rest = rest[0], rest[1:]
    out_ref, s_scr = rest
    for h in range(LOCAL_HEADS):
        for i in range(Q_BLOCKS):
            lanes = slice(i * PAIR, (i + 1) * PAIR)
            qs = q_ref[h, lanes, :]
            dos = do_ref[h, lanes, :]
            if opening:
                top = jnp.full((8, PAIR), NEG_LARGE, jnp.float32)
                total = jnp.zeros((8, PAIR), jnp.float32)
                inner = jnp.zeros((8, PAIR), jnp.float32)
            else:
                top, total, inner = (state_in[h, n, :, lanes] for n in range(3))
            todo = []
            for ref, first in zip(pieces, first_blocks):
                seen = [w for w in (first, first + 1) if visible(i, w)]
                if seen:
                    todo.append((ref, seen, (seen[0] - first) * BLOCK))
            peak = top
            at = 0
            for ref, seen, row in todo:
                s = dot(ref[row : row + len(seen) * BLOCK, h * HEAD_SIZE : (h + 1) * HEAD_SIZE], qs, 1, 1)
                for n, w in enumerate(seen):
                    x = jnp.where(
                        mask_of(hit_ref, start_ref, i, w), s[n * BLOCK : (n + 1) * BLOCK] * EXP2_SCALE, NEG_LARGE
                    )
                    s_scr[h * Q_BLOCKS + i, at : at + BLOCK, :] = x
                    peak = jnp.maximum(peak, fold(x, jnp.max))
                    at += BLOCK
            if todo and not opening:
                factor = jnp.exp2(top - peak)
                total = total * factor
                inner = inner * factor
            at = 0
            for ref, seen, row in todo:
                dp = dot(
                    ref[row : row + len(seen) * BLOCK, WIDTH + h * HEAD_SIZE : WIDTH + (h + 1) * HEAD_SIZE], dos, 1, 1
                )
                for n, w in enumerate(seen):
                    x = s_scr[h * Q_BLOCKS + i, at : at + BLOCK, :].reshape(BLOCK // 8, 8, PAIR)
                    weight = jnp.exp2(x - peak[None])
                    total = total + jnp.sum(weight, axis=0)
                    inner = inner + jnp.sum(weight * dp[n * BLOCK : (n + 1) * BLOCK].reshape(BLOCK // 8, 8, PAIR), axis=0)
                    at += BLOCK
            if closing:
                top = jnp.max(peak, axis=0, keepdims=True)
                factor = jnp.exp2(peak - top)
                total = jnp.sum(total * factor, axis=0, keepdims=True)
                inner = jnp.sum(inner * factor, axis=0, keepdims=True)
                out_ref[h, 0:1, lanes] = top + jnp.log2(total)
                out_ref[h, 1:2, lanes] = inner / total
            else:
                out_ref[h, 0, :, lanes] = peak
                out_ref[h, 1, :, lanes] = total
                out_ref[h, 2, :, lanes] = inner


def stats(first_blocks, tables, pieces, state, closing):
    opening = state is None
    shape = f32(LOCAL_HEADS, 8, ROWS) if closing else f32(LOCAL_HEADS, 3, 8, ROWS)
    return call(
        functools.partial(stats_kernel, first_blocks, opening, closing),
        "stats",
        shape,
        [SMEM_SPEC] + [VMEM_SPEC] * (3 + len(pieces) + (not opening)),
        scratch=[pltpu.VMEM((LOCAL_HEADS * Q_BLOCKS, 2 * BLOCK * len(pieces), PAIR), jnp.float32)],
    )(*tables, *pieces, *(() if opening else (state,)))


def grads_kernel(first_blocks, opening, closing, *refs):
    count = len(first_blocks)
    span = 2 * BLOCK
    if closing:
        low_ref, refs = refs[0], refs[1:]
    hit_ref, start_ref, q_ref, do_ref, norm_ref = refs[:5]
    pieces = refs[5 : 5 + count]
    rest = refs[5 + count :]
    if not opening:
        dqt_in, rest = rest[0], rest[1:]
    joined = first_blocks[-1] == BACK + 2
    if joined:
        out_refs, rest = [rest[0].at[n * span : (n + 1) * span] for n in range(count)], rest[1:]
    else:
        out_refs, rest = rest[:count], rest[count:]
    if closing:
        mine_ref, send_ref, p_scr, ds_scr, dq_scr = rest
    else:
        dqt_out, p_scr, ds_scr = rest
    for h in range(LOCAL_HEADS):
        kcols = slice(h * HEAD_SIZE, (h + 1) * HEAD_SIZE)
        vcols = slice(WIDTH + h * HEAD_SIZE, WIDTH + (h + 1) * HEAD_SIZE)
        last_row = 0
        for i in range(Q_BLOCKS):
            lanes = slice(i * PAIR, (i + 1) * PAIR)
            qs = q_ref[h, lanes, :]
            dos = do_ref[h, lanes, :]
            norm = norm_ref[h, 0:1, lanes]
            delta = norm_ref[h, 1:2, lanes]
            for m, (ref, first) in enumerate(zip(pieces, first_blocks)):
                seen = [w for w in (first, first + 1) if visible(i, w)]
                for w in (first, first + 1):
                    if w not in seen:
                        at = slice(m * span + (w - first) * BLOCK, m * span + (w - first + 1) * BLOCK)
                        p_scr[h, at, lanes] = jnp.zeros((BLOCK, PAIR), jnp.bfloat16)
                        ds_scr[h, at, lanes] = jnp.zeros((BLOCK, PAIR), jnp.bfloat16)
                if not seen:
                    continue
                row = (seen[0] - first) * BLOCK
                rows = slice(row, row + len(seen) * BLOCK)
                s = dot(ref[rows, kcols], qs, 1, 1)
                dp = dot(ref[rows, vcols], dos, 1, 1)
                for n, w in enumerate(seen):
                    part = slice(n * BLOCK, (n + 1) * BLOCK)
                    x = jnp.where(mask_of(hit_ref, start_ref, i, w), s[part] * EXP2_SCALE - norm, NEG_LARGE)
                    prob = jnp.exp2(x)
                    at = slice(m * span + (w - first) * BLOCK, m * span + (w - first + 1) * BLOCK)
                    p_scr[h, at, lanes] = prob.astype(jnp.bfloat16)
                    ds_scr[h, at, lanes] = ((prob * SCORE_SCALE) * (dp[part] - delta)).astype(jnp.bfloat16)
        keys = [ref[:, kcols] for ref in pieces]
        keys = keys[0] if count == 1 else jnp.concatenate(keys, axis=0)
        ds = ds_scr[h]
        dv = dot(p_scr[h], do_ref[h], 1, 0)
        dk = dot(ds, q_ref[h], 1, 0)
        dqt = dot(keys, ds, 0, 0)
        if not opening:
            dqt = dqt + dqt_in[h]
        for m, out in enumerate(out_refs):
            out[:, kcols] = dk[m * span : (m + 1) * span].astype(out.dtype)
            out[:, vcols] = dv[m * span : (m + 1) * span].astype(out.dtype)
        if closing:
            for b in range(2 * Q_BLOCKS):
                c = h * PAIR + (b % 2) * BLOCK
                dq_scr[b // 2 * BLOCK : (b // 2 + 1) * BLOCK, c : c + BLOCK] = dqt[:, b * BLOCK : (b + 1) * BLOCK].T
        else:
            dqt_out[h] = dqt
    if closing:
        low = low_ref[0]
        mine_ref[...] = dq_scr[pl.ds(pl.multiple_of(low * SPAN, SPAN), SPAN), :]
        send_ref[...] = dq_scr[pl.ds(pl.multiple_of((1 - low) * SPAN, SPAN), SPAN), :]


def grads(first_blocks, tables, norm, pieces, dqt, dtypes, low=None):
    opening, closing = dqt is None, low is not None
    count = len(pieces)
    rows = SPAN * count // len(dtypes)
    outs = [jax.ShapeDtypeStruct((rows, 2 * WIDTH), d) for d in dtypes]
    outs += [f32(SPAN, 2 * WIDTH)] * 2 if closing else [f32(LOCAL_HEADS, HEAD_SIZE, ROWS)]
    scratch = [pltpu.VMEM((LOCAL_HEADS, SPAN * count, ROWS), jnp.bfloat16)] * 2
    if closing:
        scratch.append(pltpu.VMEM((SLAB, 2 * WIDTH), jnp.float32))
    operands = tables + (norm,) + tuple(pieces) + (() if opening else (dqt,))
    specs = [SMEM_SPEC] + [VMEM_SPEC] * (len(operands) - 1)
    if closing:
        operands, specs = (low,) + operands, [SMEM_SPEC] + specs
    aliases = {} if opening or closing else {len(operands) - 1: len(dtypes)}
    return call(
        functools.partial(grads_kernel, first_blocks, opening, closing),
        "grads",
        tuple(outs),
        specs,
        scratch=scratch,
        aliases=aliases,
    )(*operands)


def per_device(queries, output_gradient, key_states, value_inputs, turn_ids, listed):
    slab = lax.axis_index(SLAB_AXES)
    low = lax.axis_index("xl")
    group = lax.axis_index("xh")
    low_ref = low.reshape(1)

    kv = pl.pallas_call(
        pack_kernel,
        out_shape=bf16(8, SPAN // 4, 2 * WIDTH),
        in_specs=[pl.BlockSpec(memory_space=pl.ANY)] * 2,
        out_specs=VMEM_SPEC,
        scratch_shapes=[pltpu.VMEM((SPAN // 4, KEY_VALUE_HEADS * HEAD_SIZE), jnp.bfloat16)] * 2
        + [pltpu.SemaphoreType.DMA((2,))],
        name="pack",
    )(key_states, value_inputs)
    own = lax.all_to_all(kv, MEMBER_AXES, 0, 0, tiled=True)
    b0 = own[4:].reshape(SPAN, 2 * WIDTH)
    a0 = own[:4].reshape(SPAN, 2 * WIDTH)

    b1 = slab_shift(b0, 1)
    a1 = slab_shift(a0, 1)
    b2 = slab_shift(b1, 1)
    a2 = slab_shift(a1, 1)
    send = jnp.stack(
        [lax.dynamic_slice_in_dim(x, (1 - low) * 2 * WIDTH, 2 * WIDTH, 1) for x in (queries, output_gradient)]
    )
    other = low_swap(send)
    q, do = call(
        rows_kernel, "rows", (bf16(LOCAL_HEADS, ROWS, HEAD_SIZE),) * 2, [SMEM_SPEC] + [VMEM_SPEC] * 3
    )(low_ref, queries, output_gradient, other)

    padded = jnp.concatenate([jnp.full((HALO,), -1, turn_ids.dtype), turn_ids])
    window_turns = lax.dynamic_slice_in_dim(padded, slab * SLAB, WINDOW, 0)
    start = jnp.sum((window_turns[None, :] < window_turns[HALO:, None]).astype(jnp.int32), axis=1)[None, :]
    table = lax.dynamic_index_in_dim(listed, group, 0, keepdims=False)
    table = lax.dynamic_slice_in_dim(table, slab * Q_BLOCKS, Q_BLOCKS, 0)[:, ::-1]
    key_block = slab * Q_BLOCKS - BACK + jnp.arange(Q_BLOCKS)[:, None] + jnp.arange(BACK)[None, :]
    hit = jnp.where(key_block >= 0, table, 0)
    tables = (hit, start, q, do)

    state = stats((14, 16, 10, 12), tables, (a0, b0, a1, b1), None, False)
    b2, state = lax.optimization_barrier((b2, state))
    b3 = slab_shift(b2, 1)
    a3 = slab_shift(a2, 1)
    state = stats((6, 8), tables, (a2, b2), state, False)
    b3, state = lax.optimization_barrier((b3, state))
    b4 = slab_shift(b3, 1)
    state = stats((2, 4), tables, (a3, b3), state, False)
    b4, state = lax.optimization_barrier((b4, state))
    norm = stats((0,), tables, (b4,), state, True)

    low16, full = jnp.bfloat16, jnp.float32
    def after(arrived, *values):
        return lax.optimization_barrier((arrived,) + values)[1:]

    def to_owners(x):
        return lax.all_to_all(x.reshape(8, SPAN // 4, 2 * WIDTH), MEMBER_AXES, 0, 0, tiled=True)

    def summed(part, arrived):
        return (part + arrived.astype(full)).astype(low16)

    def summed(part, arrived):
        return (part + arrived.astype(full)).astype(low16)

    gb4, dqt = grads((0,), tables, norm, (b4,), None, (low16,))
    rb = slab_shift(gb4, -1)
    ga3, gb3, dqt = grads((2, 4), tables, norm, (a3, b3), dqt, (low16, full))
    ra = slab_shift(ga3, -1)
    (dqt,) = after(rb, dqt)
    rb = slab_shift(summed(gb3, rb), -1)
    ga2, gb2, dqt = grads((6, 8), tables, norm, (a2, b2), dqt, (full, full))
    dqt, ra = lax.optimization_barrier((dqt, ra))
    ra = slab_shift(summed(ga2, ra), -1)
    g0, dqt = grads((14, 16), tables, norm, (a0, b0), dqt, (full,))
    dqt, rb = lax.optimization_barrier((dqt, rb))
    rb = slab_shift(summed(gb2, rb), -1)
    ga1, gb1, mine, send = grads((10, 12), tables, norm, (a1, b1), dqt, (full, full), low_ref)
    ra = slab_shift(summed(ga1, ra), -1)
    other = low_swap(send)
    rb = slab_shift(summed(gb1, rb), -1)
    other, rb = lax.optimization_barrier((other, rb))
    total = to_owners(g0 + jnp.concatenate([ra, rb], axis=0).astype(full))
    grad_keys, grad_values = call(
        unpack_kernel, "unpack", (f32(SPAN // 4, KEY_VALUE_HEADS * HEAD_SIZE),) * 2, [VMEM_SPEC]
    )(total)

    grad_queries = call(
        columns_kernel, "columns", f32(SPAN, 4 * WIDTH), [SMEM_SPEC] + [VMEM_SPEC] * 2
    )(low_ref, mine, other)
    return grad_queries, grad_keys, grad_values


def solution(mesh):
    fine = Mesh(mesh.devices.reshape(4, 8, 2, 2, 2), ("y", "z", "xl", "xh", "core"))
    pb, ka = ("y", "z", "xl"), ("xh", "core")
    in_specs = (P(pb, ka), P(pb, ka), P(pb + ka, None), P(pb + ka, None), P(), P())
    out_specs = (P(pb, ka), P(pb + ka, None), P(pb + ka, None))
    return jax.shard_map(per_device, mesh=fine, in_specs=in_specs, out_specs=out_specs, check_vma=False)
```

```python
import functools
import math

import jax
import jax.numpy as jnp
from jax import lax
from jax.experimental import pallas as pl
from jax.experimental.pallas import tpu as pltpu
from jax.sharding import Mesh
from jax.sharding import PartitionSpec as P

KEY_VALUE_HEADS = 16
HEAD_SIZE = 128
BLOCK = 128
BACK = 14
SPAN = 256
SLAB = 2 * SPAN
HALO = BACK * BLOCK
WINDOW = HALO + SLAB
LOCAL_HEADS = 2
WIDTH = LOCAL_HEADS * HEAD_SIZE
Q_BLOCKS = SLAB // BLOCK
PAIR = 2 * BLOCK
ROWS = Q_BLOCKS * PAIR

SCORE_SCALE = 1.0 / 12.0
EXP2_SCALE = SCORE_SCALE * math.log2(math.e)
NEG_LARGE = -1e30

SLAB_AXES = ("y", "z")
MEMBER_AXES = ("xl", "xh", "core")

VMEM_SPEC = pl.BlockSpec(memory_space=pltpu.VMEM)
SMEM_SPEC = pl.BlockSpec(memory_space=pltpu.SMEM)


def slab_shift(x, by):
    count = lax.axis_size(SLAB_AXES)
    return lax.ppermute(x, SLAB_AXES, [(i, i + by) for i in range(count) if 0 <= i + by < count])


def low_swap(x):
    return lax.ppermute(x, "xl", [(0, 1), (1, 0)])


def dot(a, b, da, db):
    return lax.dot_general(a, b, (((da,), (db,)), ((), ())), preferred_element_type=jnp.float32)


def call(kernel, name, out_shape, in_specs, scratch=(), aliases=None):
    outs = out_shape if isinstance(out_shape, (tuple, list)) else (out_shape,)
    size = sum(o.size * o.dtype.itemsize for o in outs)
    return pl.pallas_call(
        kernel,
        out_shape=out_shape,
        in_specs=in_specs,
        out_specs=jax.tree.map(lambda _: VMEM_SPEC, out_shape),
        scratch_shapes=scratch,
        input_output_aliases=aliases or {},
        compiler_params=pltpu.CompilerParams(vmem_limit_bytes=32 * 1024 * 1024),
        cost_estimate=pl.CostEstimate(flops=1024, bytes_accessed=size, transcendentals=0),
        name=name,
    )


def f32(*shape):
    return jax.ShapeDtypeStruct(shape, jnp.float32)


def bf16(*shape):
    return jax.ShapeDtypeStruct(shape, jnp.bfloat16)


def owner_columns(d):
    return (d % 4 * 4 + d // 4 * 2) * HEAD_SIZE


def pack_kernel(k_ref, v_ref, out_ref, k_scr, v_scr, sems):
    copies = [pltpu.make_async_copy(k_ref, k_scr, sems.at[0]), pltpu.make_async_copy(v_ref, v_scr, sems.at[1])]
    for copy in copies:
        copy.start()
    for n, (copy, scr) in enumerate(zip(copies, (k_scr, v_scr))):
        copy.wait()
        for d in range(8):
            c = owner_columns(d)
            out_ref[d, :, n * WIDTH : (n + 1) * WIDTH] = scr[:, c : c + WIDTH]


def unpack_kernel(in_ref, dk_ref, dv_ref):
    for d in range(8):
        c = owner_columns(d)
        dk_ref[:, c : c + WIDTH] = in_ref[d, :, :WIDTH].astype(jnp.float32)
        dv_ref[:, c : c + WIDTH] = in_ref[d, :, WIDTH:].astype(jnp.float32)


def rows_kernel(low_ref, q_ref, do_ref, other_ref, qr_ref, dor_ref):
    low = low_ref[0]
    for x, (src, dst) in enumerate(((q_ref, qr_ref), (do_ref, dor_ref))):
        for h in range(LOCAL_HEADS):
            for b in range(2):
                for n in range(2):
                    c = h * PAIR + n * BLOCK
                    rows = slice(b * BLOCK, (b + 1) * BLOCK)
                    here = pl.multiple_of((2 * low + b) * PAIR + n * BLOCK, BLOCK)
                    there = pl.multiple_of((2 * (1 - low) + b) * PAIR + n * BLOCK, BLOCK)
                    lane = pl.multiple_of(low * 2 * WIDTH + c, BLOCK)
                    dst[h, pl.ds(here, BLOCK), :] = src[rows, pl.ds(lane, BLOCK)]
                    dst[h, pl.ds(there, BLOCK), :] = other_ref[x, rows, c : c + BLOCK]


def columns_kernel(low_ref, mine_ref, other_ref, out_ref):
    low = low_ref[0]
    out_ref[:, pl.ds(pl.multiple_of(low * 2 * WIDTH, BLOCK), 2 * WIDTH)] = mine_ref[...]
    out_ref[:, pl.ds(pl.multiple_of((1 - low) * 2 * WIDTH, BLOCK), 2 * WIDTH)] = other_ref[...].astype(jnp.float32)


def visible(i, w):
    return i <= w <= i + BACK


def mask_of(hit_ref, start_ref, i, w):
    key_iota = lax.broadcasted_iota(jnp.int32, (BLOCK, BLOCK), 0)
    bound = start_ref[0:1, i * BLOCK : (i + 1) * BLOCK] - w * BLOCK
    if w < i + BACK:
        ok = key_iota >= jnp.where(hit_ref[i, w - i] > 0, -1, bound)
    else:
        ok = (key_iota >= bound) & (key_iota <= lax.broadcasted_iota(jnp.int32, (BLOCK, BLOCK), 1))
    return ok


def masked(ok, x):
    return jnp.concatenate(
        [jnp.where(ok, x[:, :BLOCK], NEG_LARGE), jnp.where(ok, x[:, BLOCK:], NEG_LARGE)], axis=1
    )


def fold(x, op):
    return op(x.reshape(BLOCK // 8, 8, PAIR), axis=0)


def stats_kernel(first_blocks, opening, closing, *refs):
    count = len(first_blocks)
    hit_ref, start_ref, q_ref, do_ref = refs[:4]
    pieces = refs[4 : 4 + count]
    rest = refs[4 + count :]
    if opening:
        state_in, rest = None, rest
    else:
        state_in, rest = rest[0], rest[1:]
    (out_ref,) = rest
    for h in range(LOCAL_HEADS):
        for i in range(Q_BLOCKS):
            lanes = slice(i * PAIR, (i + 1) * PAIR)
            qs = q_ref[h, lanes, :]
            dos = do_ref[h, lanes, :]
            if opening:
                top = jnp.full((8, PAIR), NEG_LARGE, jnp.float32)
                total = jnp.zeros((8, PAIR), jnp.float32)
                inner = jnp.zeros((8, PAIR), jnp.float32)
            else:
                top, total, inner = (state_in[h, n, :, lanes] for n in range(3))
            todo = []
            for ref, first in zip(pieces, first_blocks):
                seen = [w for w in (first, first + 1) if visible(i, w)]
                if seen:
                    todo.append((ref, seen, (seen[0] - first) * BLOCK))
            peak = top
            for ref, seen, row in todo:
                rows = slice(row, row + len(seen) * BLOCK)
                s = dot(ref[rows, h * HEAD_SIZE : (h + 1) * HEAD_SIZE], qs, 1, 1)
                dp = dot(ref[rows, WIDTH + h * HEAD_SIZE : WIDTH + (h + 1) * HEAD_SIZE], dos, 1, 1)
                for n, w in enumerate(seen):
                    part = slice(n * BLOCK, (n + 1) * BLOCK)
                    x = masked(mask_of(hit_ref, start_ref, i, w), s[part] * EXP2_SCALE)
                    higher = jnp.maximum(peak, fold(x, jnp.max))
                    weight = jnp.exp2(x.reshape(BLOCK // 8, 8, PAIR) - higher[None])
                    factor = jnp.exp2(peak - higher)
                    total = total * factor + jnp.sum(weight, axis=0)
                    inner = inner * factor + jnp.sum(weight * dp[part].reshape(BLOCK // 8, 8, PAIR), axis=0)
                    peak = higher
            if closing:
                top = jnp.max(peak, axis=0, keepdims=True)
                factor = jnp.exp2(peak - top)
                total = jnp.sum(total * factor, axis=0, keepdims=True)
                inner = jnp.sum(inner * factor, axis=0, keepdims=True)
                out_ref[h, 0:1, lanes] = top + jnp.log2(total)
                out_ref[h, 1:2, lanes] = inner / total
            else:
                out_ref[h, 0, :, lanes] = peak
                out_ref[h, 1, :, lanes] = total
                out_ref[h, 2, :, lanes] = inner


def stats(first_blocks, tables, pieces, state, closing):
    opening = state is None
    shape = f32(LOCAL_HEADS, 8, ROWS) if closing else f32(LOCAL_HEADS, 3, 8, ROWS)
    return call(
        functools.partial(stats_kernel, first_blocks, opening, closing),
        "stats",
        shape,
        [SMEM_SPEC] + [VMEM_SPEC] * (3 + len(pieces) + (not opening)),
    )(*tables, *pieces, *(() if opening else (state,)))


def grads_kernel(first_blocks, opening, closing, *refs):
    count = len(first_blocks)
    span = 2 * BLOCK
    if closing:
        low_ref, refs = refs[0], refs[1:]
    hit_ref, start_ref, q_ref, do_ref, norm_ref = refs[:5]
    pieces = refs[5 : 5 + count]
    rest = refs[5 + count :]
    if not opening:
        dqt_in, rest = rest[0], rest[1:]
    joined = first_blocks[-1] == BACK + 2
    if joined:
        out_refs, rest = [rest[0].at[n * span : (n + 1) * span] for n in range(count)], rest[1:]
    else:
        out_refs, rest = rest[:count], rest[count:]
    if closing:
        mine_ref, send_ref, p_scr, ds_scr, dq_scr = rest
    else:
        dqt_out, p_scr, ds_scr = rest
    for h in range(LOCAL_HEADS):
        kcols = slice(h * HEAD_SIZE, (h + 1) * HEAD_SIZE)
        vcols = slice(WIDTH + h * HEAD_SIZE, WIDTH + (h + 1) * HEAD_SIZE)
        last_row = 0
        for i in range(Q_BLOCKS):
            lanes = slice(i * PAIR, (i + 1) * PAIR)
            qs = q_ref[h, lanes, :]
            dos = do_ref[h, lanes, :]
            norm = norm_ref[h, 0:1, lanes]
            delta = norm_ref[h, 1:2, lanes]
            for m, (ref, first) in enumerate(zip(pieces, first_blocks)):
                seen = [w for w in (first, first + 1) if visible(i, w)]
                for w in (first, first + 1):
                    if w not in seen:
                        at = slice(m * span + (w - first) * BLOCK, m * span + (w - first + 1) * BLOCK)
                        p_scr[h, at, lanes] = jnp.zeros((BLOCK, PAIR), jnp.bfloat16)
                        ds_scr[h, at, lanes] = jnp.zeros((BLOCK, PAIR), jnp.bfloat16)
                if not seen:
                    continue
                row = (seen[0] - first) * BLOCK
                rows = slice(row, row + len(seen) * BLOCK)
                s = dot(ref[rows, kcols], qs, 1, 1)
                dp = dot(ref[rows, vcols], dos, 1, 1)
                for n, w in enumerate(seen):
                    part = slice(n * BLOCK, (n + 1) * BLOCK)
                    x = masked(mask_of(hit_ref, start_ref, i, w), s[part] * EXP2_SCALE - norm)
                    prob = jnp.exp2(x)
                    at = slice(m * span + (w - first) * BLOCK, m * span + (w - first + 1) * BLOCK)
                    p_scr[h, at, lanes] = prob.astype(jnp.bfloat16)
                    ds_scr[h, at, lanes] = ((prob * SCORE_SCALE) * (dp[part] - delta)).astype(jnp.bfloat16)
        keys = [ref[:, kcols] for ref in pieces]
        keys = keys[0] if count == 1 else jnp.concatenate(keys, axis=0)
        ds = ds_scr[h]
        dv = dot(p_scr[h], do_ref[h], 1, 0)
        dk = dot(ds, q_ref[h], 1, 0)
        dqt = dot(keys, ds, 0, 0)
        if not opening:
            dqt = dqt + dqt_in[h]
        for m, out in enumerate(out_refs):
            out[:, kcols] = dk[m * span : (m + 1) * span].astype(out.dtype)
            out[:, vcols] = dv[m * span : (m + 1) * span].astype(out.dtype)
        if closing:
            for b in range(2 * Q_BLOCKS):
                c = h * PAIR + (b % 2) * BLOCK
                dq_scr[b // 2 * BLOCK : (b // 2 + 1) * BLOCK, c : c + BLOCK] = dqt[:, b * BLOCK : (b + 1) * BLOCK].T
        else:
            dqt_out[h] = dqt
    if closing:
        low = low_ref[0]
        mine_ref[...] = dq_scr[pl.ds(pl.multiple_of(low * SPAN, SPAN), SPAN), :]
        send_ref[...] = dq_scr[pl.ds(pl.multiple_of((1 - low) * SPAN, SPAN), SPAN), :].astype(jnp.bfloat16)


def grads(first_blocks, tables, norm, pieces, dqt, dtypes, low=None):
    opening, closing = dqt is None, low is not None
    count = len(pieces)
    rows = SPAN * count // len(dtypes)
    outs = [jax.ShapeDtypeStruct((rows, 2 * WIDTH), d) for d in dtypes]
    outs += [f32(SPAN, 2 * WIDTH), bf16(SPAN, 2 * WIDTH)] if closing else [f32(LOCAL_HEADS, HEAD_SIZE, ROWS)]
    scratch = [pltpu.VMEM((LOCAL_HEADS, SPAN * count, ROWS), jnp.bfloat16)] * 2
    if closing:
        scratch.append(pltpu.VMEM((SLAB, 2 * WIDTH), jnp.float32))
    operands = tables + (norm,) + tuple(pieces) + (() if opening else (dqt,))
    specs = [SMEM_SPEC] + [VMEM_SPEC] * (len(operands) - 1)
    if closing:
        operands, specs = (low,) + operands, [SMEM_SPEC] + specs
    aliases = {} if opening or closing else {len(operands) - 1: len(dtypes)}
    return call(
        functools.partial(grads_kernel, first_blocks, opening, closing),
        "grads",
        tuple(outs),
        specs,
        scratch=scratch,
        aliases=aliases,
    )(*operands)


def per_device(queries, output_gradient, key_states, value_inputs, turn_ids, listed):
    slab = lax.axis_index(SLAB_AXES)
    low = lax.axis_index("xl")
    group = lax.axis_index("xh")
    low_ref = low.reshape(1)

    kv = pl.pallas_call(
        pack_kernel,
        out_shape=bf16(8, SPAN // 4, 2 * WIDTH),
        in_specs=[pl.BlockSpec(memory_space=pl.ANY)] * 2,
        out_specs=VMEM_SPEC,
        scratch_shapes=[pltpu.VMEM((SPAN // 4, KEY_VALUE_HEADS * HEAD_SIZE), jnp.bfloat16)] * 2
        + [pltpu.SemaphoreType.DMA((2,))],
        name="pack",
    )(key_states, value_inputs)
    own = lax.all_to_all(kv, MEMBER_AXES, 0, 0, tiled=True)
    b0 = own[4:].reshape(SPAN, 2 * WIDTH)
    a0 = own[:4].reshape(SPAN, 2 * WIDTH)

    b1 = slab_shift(b0, 1)
    a1 = slab_shift(a0, 1)
    b2 = slab_shift(b1, 1)
    a2 = slab_shift(a1, 1)
    send = jnp.stack(
        [lax.dynamic_slice_in_dim(x, (1 - low) * 2 * WIDTH, 2 * WIDTH, 1) for x in (queries, output_gradient)]
    )
    other = low_swap(send)
    q, do = call(
        rows_kernel, "rows", (bf16(LOCAL_HEADS, ROWS, HEAD_SIZE),) * 2, [SMEM_SPEC] + [VMEM_SPEC] * 3
    )(low_ref, queries, output_gradient, other)

    padded = jnp.concatenate([jnp.full((HALO,), -1, turn_ids.dtype), turn_ids])
    window_turns = lax.dynamic_slice_in_dim(padded, slab * SLAB, WINDOW, 0)
    start = jnp.sum((window_turns[None, :] < window_turns[HALO:, None]).astype(jnp.int32), axis=1)[None, :]
    table = lax.dynamic_index_in_dim(listed, group, 0, keepdims=False)
    table = lax.dynamic_slice_in_dim(table, slab * Q_BLOCKS, Q_BLOCKS, 0)[:, ::-1]
    key_block = slab * Q_BLOCKS - BACK + jnp.arange(Q_BLOCKS)[:, None] + jnp.arange(BACK)[None, :]
    hit = jnp.where(key_block >= 0, table, 0)
    tables = (hit, start, q, do)

    state = stats((14, 16, 10, 12), tables, (a0, b0, a1, b1), None, False)
    b2, state = lax.optimization_barrier((b2, state))
    b3 = slab_shift(b2, 1)
    a3 = slab_shift(a2, 1)
    state = stats((6, 8), tables, (a2, b2), state, False)
    b3, state = lax.optimization_barrier((b3, state))
    b4 = slab_shift(b3, 1)
    state = stats((2, 4), tables, (a3, b3), state, False)
    b4, state = lax.optimization_barrier((b4, state))
    norm = stats((0,), tables, (b4,), state, True)

    low16, full = jnp.bfloat16, jnp.float32
    def after(arrived, *values):
        return lax.optimization_barrier((arrived,) + values)[1:]

    def to_owners(x):
        return lax.all_to_all(x.reshape(8, SPAN // 4, 2 * WIDTH), MEMBER_AXES, 0, 0, tiled=True)

    def summed(part, arrived):
        return (part + arrived.astype(full)).astype(low16)

    def summed(part, arrived):
        return (part + arrived.astype(full)).astype(low16)

    gb4, dqt = grads((0,), tables, norm, (b4,), None, (low16,))
    rb = slab_shift(gb4, -1)
    ga3, gb3, dqt = grads((2, 4), tables, norm, (a3, b3), dqt, (low16, full))
    ra = slab_shift(ga3, -1)
    (dqt,) = after(rb, dqt)
    rb = slab_shift(summed(gb3, rb), -1)
    ga2, gb2, dqt = grads((6, 8), tables, norm, (a2, b2), dqt, (full, full))
    ra = slab_shift(summed(ga2, ra), -1)
    (dqt,) = after(rb, dqt)
    rb = slab_shift(summed(gb2, rb), -1)
    ga1, gb1, dqt = grads((10, 12), tables, norm, (a1, b1), dqt, (full, full))
    dqt, ra = lax.optimization_barrier((dqt, summed(ga1, ra)))
    ra = slab_shift(ra, -1)
    g0, mine, send = grads((14, 16), tables, norm, (a0, b0), dqt, (full,), low_ref)
    send, rb = lax.optimization_barrier((send, rb))
    rb = slab_shift(summed(gb1, rb), -1)
    other = low_swap(send)
    other, rb = lax.optimization_barrier((other, rb))
    total = to_owners((g0 + jnp.concatenate([ra, rb], axis=0).astype(full)).astype(low16))
    grad_keys, grad_values = call(
        unpack_kernel, "unpack", (f32(SPAN // 4, KEY_VALUE_HEADS * HEAD_SIZE),) * 2, [VMEM_SPEC]
    )(total)

    grad_queries = call(
        columns_kernel, "columns", f32(SPAN, 4 * WIDTH), [SMEM_SPEC] + [VMEM_SPEC] * 2
    )(low_ref, mine, other)
    return grad_queries, grad_keys, grad_values


def solution(mesh):
    fine = Mesh(mesh.devices.reshape(4, 8, 2, 2, 2), ("y", "z", "xl", "xh", "core"))
    pb, ka = ("y", "z", "xl"), ("xh", "core")
    in_specs = (P(pb, ka), P(pb, ka), P(pb + ka, None), P(pb + ka, None), P(), P())
    out_specs = (P(pb, ka), P(pb + ka, None), P(pb + ka, None))
    return jax.shard_map(per_device, mesh=fine, in_specs=in_specs, out_specs=out_specs, check_vma=False)
```

```python
import functools
import math

import jax
import jax.numpy as jnp
from jax import lax
from jax.experimental import pallas as pl
from jax.experimental.pallas import tpu as pltpu
from jax.sharding import Mesh
from jax.sharding import PartitionSpec as P

KEY_VALUE_HEADS = 16
HEAD_SIZE = 128
BLOCK = 128
BACK = 14
SPAN = 256
SLAB = 2 * SPAN
HALO = BACK * BLOCK
WINDOW = HALO + SLAB
LOCAL_HEADS = 2
WIDTH = LOCAL_HEADS * HEAD_SIZE
Q_BLOCKS = SLAB // BLOCK
PAIR = 2 * BLOCK
ROWS = Q_BLOCKS * PAIR

SCORE_SCALE = 1.0 / 12.0
EXP2_SCALE = SCORE_SCALE * math.log2(math.e)
NEG_LARGE = -1e30

SLAB_AXES = ("y", "z")
MEMBER_AXES = ("xl", "xh", "core")

VMEM_SPEC = pl.BlockSpec(memory_space=pltpu.VMEM)
SMEM_SPEC = pl.BlockSpec(memory_space=pltpu.SMEM)


def slab_shift(x, by):
    count = lax.axis_size(SLAB_AXES)
    return lax.ppermute(x, SLAB_AXES, [(i, i + by) for i in range(count) if 0 <= i + by < count])


def low_swap(x):
    return lax.ppermute(x, "xl", [(0, 1), (1, 0)])


def dot(a, b, da, db):
    return lax.dot_general(a, b, (((da,), (db,)), ((), ())), preferred_element_type=jnp.float32)


def call(kernel, name, out_shape, in_specs, scratch=(), aliases=None, light=False):
    outs = out_shape if isinstance(out_shape, (tuple, list)) else (out_shape,)
    size = sum(o.size * o.dtype.itemsize for o in outs)
    return pl.pallas_call(
        kernel,
        out_shape=out_shape,
        in_specs=in_specs,
        out_specs=jax.tree.map(lambda _: VMEM_SPEC, out_shape),
        scratch_shapes=scratch,
        input_output_aliases=aliases or {},
        compiler_params=pltpu.CompilerParams(vmem_limit_bytes=32 * 1024 * 1024),
        cost_estimate=pl.CostEstimate(flops=1024, bytes_accessed=1 if light else size, transcendentals=0),
        name=name,
    )


def f32(*shape):
    return jax.ShapeDtypeStruct(shape, jnp.float32)


def bf16(*shape):
    return jax.ShapeDtypeStruct(shape, jnp.bfloat16)


def owner_columns(d):
    return (d % 4 * 4 + d // 4 * 2) * HEAD_SIZE


def pack_kernel(k_ref, v_ref, out_ref, k_scr, v_scr, sems):
    copies = [pltpu.make_async_copy(k_ref, k_scr, sems.at[0]), pltpu.make_async_copy(v_ref, v_scr, sems.at[1])]
    for copy in copies:
        copy.start()
    for n, (copy, scr) in enumerate(zip(copies, (k_scr, v_scr))):
        copy.wait()
        for d in range(8):
            c = owner_columns(d)
            out_ref[d, :, n * WIDTH : (n + 1) * WIDTH] = scr[:, c : c + WIDTH]


def unpack_kernel(in_ref, dk_ref, dv_ref):
    for d in range(8):
        c = owner_columns(d)
        dk_ref[:, c : c + WIDTH] = in_ref[d, :, :WIDTH].astype(jnp.float32)
        dv_ref[:, c : c + WIDTH] = in_ref[d, :, WIDTH:].astype(jnp.float32)


def rows_kernel(low_ref, q_ref, do_ref, other_ref, qr_ref, dor_ref):
    low = low_ref[0]
    for x, (src, dst) in enumerate(((q_ref, qr_ref), (do_ref, dor_ref))):
        for h in range(LOCAL_HEADS):
            for b in range(2):
                for n in range(2):
                    c = h * PAIR + n * BLOCK
                    rows = slice(b * BLOCK, (b + 1) * BLOCK)
                    here = pl.multiple_of((2 * low + b) * PAIR + n * BLOCK, BLOCK)
                    there = pl.multiple_of((2 * (1 - low) + b) * PAIR + n * BLOCK, BLOCK)
                    lane = pl.multiple_of(low * 2 * WIDTH + c, BLOCK)
                    dst[h, pl.ds(here, BLOCK), :] = src[rows, pl.ds(lane, BLOCK)]
                    dst[h, pl.ds(there, BLOCK), :] = other_ref[x, rows, c : c + BLOCK]


def columns_kernel(low_ref, mine_ref, other_ref, out_ref):
    low = low_ref[0]
    out_ref[:, pl.ds(pl.multiple_of(low * 2 * WIDTH, BLOCK), 2 * WIDTH)] = mine_ref[...]
    out_ref[:, pl.ds(pl.multiple_of((1 - low) * 2 * WIDTH, BLOCK), 2 * WIDTH)] = other_ref[...].astype(jnp.float32)


def visible(i, w):
    return i <= w <= i + BACK


def mask_of(hit_ref, start_ref, i, w):
    key_iota = lax.broadcasted_iota(jnp.int32, (BLOCK, BLOCK), 0)
    bound = start_ref[0:1, i * BLOCK : (i + 1) * BLOCK] - w * BLOCK
    if w < i + BACK:
        ok = key_iota >= jnp.where(hit_ref[i, w - i] > 0, -1, bound)
    else:
        ok = (key_iota >= bound) & (key_iota <= lax.broadcasted_iota(jnp.int32, (BLOCK, BLOCK), 1))
    return ok


def masked(ok, x):
    return jnp.concatenate(
        [jnp.where(ok, x[:, :BLOCK], NEG_LARGE), jnp.where(ok, x[:, BLOCK:], NEG_LARGE)], axis=1
    )


def fold(x, op):
    return op(x.reshape(BLOCK // 8, 8, PAIR), axis=0)


def stats_kernel(first_blocks, opening, closing, *refs):
    count = len(first_blocks)
    hit_ref, start_ref, q_ref, do_ref = refs[:4]
    pieces = refs[4 : 4 + count]
    rest = refs[4 + count :]
    if opening:
        state_in, rest = None, rest
    else:
        state_in, rest = rest[0], rest[1:]
    (out_ref,) = rest
    for h in range(LOCAL_HEADS):
        for i in range(Q_BLOCKS):
            lanes = slice(i * PAIR, (i + 1) * PAIR)
            qs = q_ref[h, lanes, :]
            dos = do_ref[h, lanes, :]
            if opening:
                top = jnp.full((8, PAIR), NEG_LARGE, jnp.float32)
                total = jnp.zeros((8, PAIR), jnp.float32)
                inner = jnp.zeros((8, PAIR), jnp.float32)
            else:
                top, total, inner = (state_in[h, n, :, lanes] for n in range(3))
            todo = []
            for ref, first in zip(pieces, first_blocks):
                seen = [w for w in (first, first + 1) if visible(i, w)]
                if seen:
                    todo.append((ref, seen, (seen[0] - first) * BLOCK))
            peak = top
            for ref, seen, row in todo:
                rows = slice(row, row + len(seen) * BLOCK)
                s = dot(ref[rows, h * HEAD_SIZE : (h + 1) * HEAD_SIZE], qs, 1, 1)
                dp = dot(ref[rows, WIDTH + h * HEAD_SIZE : WIDTH + (h + 1) * HEAD_SIZE], dos, 1, 1)
                for n, w in enumerate(seen):
                    part = slice(n * BLOCK, (n + 1) * BLOCK)
                    x = masked(mask_of(hit_ref, start_ref, i, w), s[part] * EXP2_SCALE)
                    higher = jnp.maximum(peak, fold(x, jnp.max))
                    weight = jnp.exp2(x.reshape(BLOCK // 8, 8, PAIR) - higher[None])
                    factor = jnp.exp2(peak - higher)
                    total = total * factor + jnp.sum(weight, axis=0)
                    inner = inner * factor + jnp.sum(weight * dp[part].reshape(BLOCK // 8, 8, PAIR), axis=0)
                    peak = higher
            if closing:
                top = jnp.max(peak, axis=0, keepdims=True)
                factor = jnp.exp2(peak - top)
                total = jnp.sum(total * factor, axis=0, keepdims=True)
                inner = jnp.sum(inner * factor, axis=0, keepdims=True)
                out_ref[h, 0:1, lanes] = top + jnp.log2(total)
                out_ref[h, 1:2, lanes] = inner / total
            else:
                out_ref[h, 0, :, lanes] = peak
                out_ref[h, 1, :, lanes] = total
                out_ref[h, 2, :, lanes] = inner


def stats(first_blocks, tables, pieces, state, closing):
    opening = state is None
    shape = f32(LOCAL_HEADS, 8, ROWS) if closing else f32(LOCAL_HEADS, 3, 8, ROWS)
    return call(
        functools.partial(stats_kernel, first_blocks, opening, closing),
        "stats",
        shape,
        [SMEM_SPEC] + [VMEM_SPEC] * (3 + len(pieces) + (not opening)),
    )(*tables, *pieces, *(() if opening else (state,)))


def grads_kernel(first_blocks, opening, closing, *refs):
    count = len(first_blocks)
    span = 2 * BLOCK
    query_blocks = min(Q_BLOCKS, first_blocks[-1] + 2)
    rows_used = query_blocks * PAIR
    if closing:
        low_ref, refs = refs[0], refs[1:]
    hit_ref, start_ref, q_ref, do_ref, norm_ref = refs[:5]
    pieces = refs[5 : 5 + count]
    rest = refs[5 + count :]
    if not opening:
        dqt_in, rest = rest[0], rest[1:]
    joined = first_blocks[-1] == BACK + 2
    if joined:
        out_refs, rest = [rest[0].at[n * span : (n + 1) * span] for n in range(count)], rest[1:]
    else:
        out_refs, rest = rest[:count], rest[count:]
    if closing:
        mine_ref, send_ref, p_scr, ds_scr, dq_scr = rest
    else:
        dqt_out, p_scr, ds_scr = rest
    for h in range(LOCAL_HEADS):
        kcols = slice(h * HEAD_SIZE, (h + 1) * HEAD_SIZE)
        vcols = slice(WIDTH + h * HEAD_SIZE, WIDTH + (h + 1) * HEAD_SIZE)
        for i in range(query_blocks):
            lanes = slice(i * PAIR, (i + 1) * PAIR)
            qs = q_ref[h, lanes, :]
            dos = do_ref[h, lanes, :]
            norm = norm_ref[h, 0:1, lanes]
            delta = norm_ref[h, 1:2, lanes]
            for m, (ref, first) in enumerate(zip(pieces, first_blocks)):
                seen = [w for w in (first, first + 1) if visible(i, w)]
                for w in (first, first + 1):
                    if w not in seen:
                        at = slice(m * span + (w - first) * BLOCK, m * span + (w - first + 1) * BLOCK)
                        p_scr[h, at, lanes] = jnp.zeros((BLOCK, PAIR), jnp.bfloat16)
                        ds_scr[h, at, lanes] = jnp.zeros((BLOCK, PAIR), jnp.bfloat16)
                if not seen:
                    continue
                row = (seen[0] - first) * BLOCK
                rows = slice(row, row + len(seen) * BLOCK)
                s = dot(ref[rows, kcols], qs, 1, 1)
                dp = dot(ref[rows, vcols], dos, 1, 1)
                for n, w in enumerate(seen):
                    part = slice(n * BLOCK, (n + 1) * BLOCK)
                    x = masked(mask_of(hit_ref, start_ref, i, w), s[part] * EXP2_SCALE - norm)
                    prob = jnp.exp2(x)
                    at = slice(m * span + (w - first) * BLOCK, m * span + (w - first + 1) * BLOCK)
                    p_scr[h, at, lanes] = prob.astype(jnp.bfloat16)
                    ds_scr[h, at, lanes] = ((prob * SCORE_SCALE) * (dp[part] - delta)).astype(jnp.bfloat16)
        keys = [ref[:, kcols] for ref in pieces]
        keys = keys[0] if count == 1 else jnp.concatenate(keys, axis=0)
        used = slice(0, rows_used)
        ds = ds_scr[h, :, used]
        dv = dot(p_scr[h, :, used], do_ref[h, used, :], 1, 0)
        dk = dot(ds, q_ref[h, used, :], 1, 0)
        dqt = dot(keys, ds, 0, 0)
        if not opening:
            dqt = dqt + dqt_in[h]
        for m, out in enumerate(out_refs):
            out[:, kcols] = dk[m * span : (m + 1) * span].astype(out.dtype)
            out[:, vcols] = dv[m * span : (m + 1) * span].astype(out.dtype)
        if closing:
            for b in range(2 * Q_BLOCKS):
                c = h * PAIR + (b % 2) * BLOCK
                dq_scr[b // 2 * BLOCK : (b // 2 + 1) * BLOCK, c : c + BLOCK] = dqt[:, b * BLOCK : (b + 1) * BLOCK].T
        else:
            dqt_out[h, :, used] = dqt
            if rows_used < ROWS:
                dqt_out[h, :, rows_used:] = jnp.zeros((HEAD_SIZE, ROWS - rows_used), jnp.float32)
    if closing:
        low = low_ref[0]
        mine_ref[...] = dq_scr[pl.ds(pl.multiple_of(low * SPAN, SPAN), SPAN), :]
        send_ref[...] = dq_scr[pl.ds(pl.multiple_of((1 - low) * SPAN, SPAN), SPAN), :].astype(jnp.bfloat16)


def grads(first_blocks, tables, norm, pieces, dqt, dtypes, low=None, light=False):
    opening, closing = dqt is None, low is not None
    count = len(pieces)
    rows = SPAN * count // len(dtypes)
    outs = [jax.ShapeDtypeStruct((rows, 2 * WIDTH), d) for d in dtypes]
    outs += [f32(SPAN, 2 * WIDTH), bf16(SPAN, 2 * WIDTH)] if closing else [f32(LOCAL_HEADS, HEAD_SIZE, ROWS)]
    scratch = [pltpu.VMEM((LOCAL_HEADS, SPAN * count, ROWS), jnp.bfloat16)] * 2
    if closing:
        scratch.append(pltpu.VMEM((SLAB, 2 * WIDTH), jnp.float32))
    operands = tables + (norm,) + tuple(pieces) + (() if opening else (dqt,))
    specs = [SMEM_SPEC] + [VMEM_SPEC] * (len(operands) - 1)
    if closing:
        operands, specs = (low,) + operands, [SMEM_SPEC] + specs
    aliases = {} if opening or closing else {len(operands) - 1: len(dtypes)}
    return call(
        functools.partial(grads_kernel, first_blocks, opening, closing),
        "grads",
        tuple(outs),
        specs,
        scratch=scratch,
        aliases=aliases,
        light=light,
    )(*operands)


def finish_kernel(hit_ref, start_ref, q_ref, do_ref, piece, state, norm_ref, far_ref, dqt_ref, p_scr, ds_scr):
    tables = (hit_ref, start_ref, q_ref, do_ref)
    stats_kernel((0,), False, True, *tables, piece, state, norm_ref)
    grads_kernel((0,), True, False, *tables, norm_ref, piece, far_ref, dqt_ref, p_scr, ds_scr)


def finish(tables, piece, state):
    return call(
        finish_kernel,
        "finish",
        (f32(LOCAL_HEADS, 8, ROWS), bf16(SPAN, 2 * WIDTH), f32(LOCAL_HEADS, HEAD_SIZE, ROWS)),
        [SMEM_SPEC] + [VMEM_SPEC] * 5,
        scratch=[pltpu.VMEM((LOCAL_HEADS, SPAN, 2 * PAIR), jnp.bfloat16)] * 2,
    )(*tables, piece, state)


def per_device(queries, output_gradient, key_states, value_inputs, turn_ids, listed):
    slab = lax.axis_index(SLAB_AXES)
    low = lax.axis_index("xl")
    group = lax.axis_index("xh")
    low_ref = low.reshape(1)

    kv = pl.pallas_call(
        pack_kernel,
        out_shape=bf16(8, SPAN // 4, 2 * WIDTH),
        in_specs=[pl.BlockSpec(memory_space=pl.ANY)] * 2,
        out_specs=VMEM_SPEC,
        scratch_shapes=[pltpu.VMEM((SPAN // 4, KEY_VALUE_HEADS * HEAD_SIZE), jnp.bfloat16)] * 2
        + [pltpu.SemaphoreType.DMA((2,))],
        name="pack",
    )(key_states, value_inputs)
    own = lax.all_to_all(kv, MEMBER_AXES, 0, 0, tiled=True)
    b0 = own[4:].reshape(SPAN, 2 * WIDTH)
    a0 = own[:4].reshape(SPAN, 2 * WIDTH)

    b1 = slab_shift(b0, 1)
    a1 = slab_shift(a0, 1)
    b2 = slab_shift(b1, 1)
    a2 = slab_shift(a1, 1)
    send = jnp.stack(
        [lax.dynamic_slice_in_dim(x, (1 - low) * 2 * WIDTH, 2 * WIDTH, 1) for x in (queries, output_gradient)]
    )
    other = low_swap(send)
    q, do = call(
        rows_kernel, "rows", (bf16(LOCAL_HEADS, ROWS, HEAD_SIZE),) * 2, [SMEM_SPEC] + [VMEM_SPEC] * 3
    )(low_ref, queries, output_gradient, other)

    padded = jnp.concatenate([jnp.full((HALO,), -1, turn_ids.dtype), turn_ids])
    window_turns = lax.dynamic_slice_in_dim(padded, slab * SLAB, WINDOW, 0)
    start = jnp.sum((window_turns[None, :] < window_turns[HALO:, None]).astype(jnp.int32), axis=1)[None, :]
    table = lax.dynamic_index_in_dim(listed, group, 0, keepdims=False)
    table = lax.dynamic_slice_in_dim(table, slab * Q_BLOCKS, Q_BLOCKS, 0)[:, ::-1]
    key_block = slab * Q_BLOCKS - BACK + jnp.arange(Q_BLOCKS)[:, None] + jnp.arange(BACK)[None, :]
    hit = jnp.where(key_block >= 0, table, 0)
    tables = (hit, start, q, do)

    state = stats((14, 16, 10, 12), tables, (a0, b0, a1, b1), None, False)
    b2, state = lax.optimization_barrier((b2, state))
    b3 = slab_shift(b2, 1)
    a3 = slab_shift(a2, 1)
    state = stats((6, 8), tables, (a2, b2), state, False)
    b3, state = lax.optimization_barrier((b3, state))
    b4 = slab_shift(b3, 1)
    state = stats((2, 4), tables, (a3, b3), state, False)
    b4, state = lax.optimization_barrier((b4, state))
    norm, gb4, dqt = finish(tables, b4, state)

    low16, full = jnp.bfloat16, jnp.float32
    def to_owners(x):
        return lax.all_to_all(x.reshape(8, SPAN // 4, 2 * WIDTH), MEMBER_AXES, 0, 0, tiled=True)

    def summed(part, arrived):
        return (part + arrived.astype(full)).astype(low16)

    def summed(part, arrived):
        return (part + arrived.astype(full)).astype(low16)

    rb = slab_shift(gb4, -1)
    ga3, gb3, dqt = grads((2, 4), tables, norm, (a3, b3), dqt, (low16, full), light=True)
    ra = slab_shift(ga3, -1)
    g0, dqt = grads((14, 16), tables, norm, (a0, b0), dqt, (full,), light=True)
    dqt, rb = lax.optimization_barrier((dqt, rb))
    rb = slab_shift(summed(gb3, rb), -1)
    dqt, ra = lax.optimization_barrier((dqt, ra))
    ga2, gb2, dqt = grads((6, 8), tables, norm, (a2, b2), dqt, (full, full))
    ra = slab_shift(summed(ga2, ra), -1)
    dqt, rb = lax.optimization_barrier((dqt, rb))
    rb = slab_shift(summed(gb2, rb), -1)
    ga1, gb1, mine, send = grads((10, 12), tables, norm, (a1, b1), dqt, (full, full), low_ref)
    ra = slab_shift(summed(ga1, ra), -1)
    rb = slab_shift(summed(gb1, rb), -1)
    other = low_swap(send)
    other, rb = lax.optimization_barrier((other, rb))
    total = lax.dynamic_update_slice(jnp.zeros((SLAB, 2 * WIDTH), low16), summed(g0[:SPAN], ra), (0, 0))
    total, rb = lax.optimization_barrier((total, rb))
    total = to_owners(lax.dynamic_update_slice(total, summed(g0[SPAN:], rb), (SPAN, 0)))
    grad_keys, grad_values = call(
        unpack_kernel, "unpack", (f32(SPAN // 4, KEY_VALUE_HEADS * HEAD_SIZE),) * 2, [VMEM_SPEC]
    )(total)

    grad_queries = call(
        columns_kernel, "columns", f32(SPAN, 4 * WIDTH), [SMEM_SPEC] + [VMEM_SPEC] * 2
    )(low_ref, mine, other)
    return grad_queries, grad_keys, grad_values


def solution(mesh):
    fine = Mesh(mesh.devices.reshape(4, 8, 2, 2, 2), ("y", "z", "xl", "xh", "core"))
    pb, ka = ("y", "z", "xl"), ("xh", "core")
    in_specs = (P(pb, ka), P(pb, ka), P(pb + ka, None), P(pb + ka, None), P(), P())
    out_specs = (P(pb, ka), P(pb + ka, None), P(pb + ka, None))
    return jax.shard_map(per_device, mesh=fine, in_specs=in_specs, out_specs=out_specs, check_vma=False)
```

```python
import functools
import math

import jax
import jax.numpy as jnp
from jax import lax
from jax.experimental import pallas as pl
from jax.experimental.pallas import tpu as pltpu
from jax.sharding import Mesh
from jax.sharding import PartitionSpec as P

KEY_VALUE_HEADS = 16
HEAD_SIZE = 128
BLOCK = 128
BACK = 14
SPAN = 256
SLAB = 2 * SPAN
HALO = BACK * BLOCK
WINDOW = HALO + SLAB
LOCAL_HEADS = 2
WIDTH = LOCAL_HEADS * HEAD_SIZE
Q_BLOCKS = SLAB // BLOCK
PAIR = 2 * BLOCK
ROWS = Q_BLOCKS * PAIR

SCORE_SCALE = 1.0 / 12.0
EXP2_SCALE = SCORE_SCALE * math.log2(math.e)
NEG_LARGE = -1e30

SLAB_AXES = ("y", "z")
MEMBER_AXES = ("xl", "xh", "core")

VMEM_SPEC = pl.BlockSpec(memory_space=pltpu.VMEM)
SMEM_SPEC = pl.BlockSpec(memory_space=pltpu.SMEM)


def slab_shift(x, by):
    count = lax.axis_size(SLAB_AXES)
    return lax.ppermute(x, SLAB_AXES, [(i, i + by) for i in range(count) if 0 <= i + by < count])


def low_swap(x):
    return lax.ppermute(x, "xl", [(0, 1), (1, 0)])


def dot(a, b, da, db):
    return lax.dot_general(a, b, (((da,), (db,)), ((), ())), preferred_element_type=jnp.float32)


def call(kernel, name, out_shape, in_specs, scratch=(), aliases=None, light=False):
    outs = out_shape if isinstance(out_shape, (tuple, list)) else (out_shape,)
    size = sum(o.size * o.dtype.itemsize for o in outs)
    return pl.pallas_call(
        kernel,
        out_shape=out_shape,
        in_specs=in_specs,
        out_specs=jax.tree.map(lambda _: VMEM_SPEC, out_shape),
        scratch_shapes=scratch,
        input_output_aliases=aliases or {},
        compiler_params=pltpu.CompilerParams(vmem_limit_bytes=32 * 1024 * 1024),
        cost_estimate=pl.CostEstimate(flops=1024, bytes_accessed=1 if light else size, transcendentals=0),
        name=name,
    )


def f32(*shape):
    return jax.ShapeDtypeStruct(shape, jnp.float32)


def bf16(*shape):
    return jax.ShapeDtypeStruct(shape, jnp.bfloat16)


def owner_columns(d):
    return (d % 4 * 4 + d // 4 * 2) * HEAD_SIZE


def pack_kernel(k_ref, v_ref, out_ref, k_scr, v_scr, sems):
    copies = [pltpu.make_async_copy(k_ref, k_scr, sems.at[0]), pltpu.make_async_copy(v_ref, v_scr, sems.at[1])]
    for copy in copies:
        copy.start()
    for n, (copy, scr) in enumerate(zip(copies, (k_scr, v_scr))):
        copy.wait()
        for d in range(8):
            c = owner_columns(d)
            out_ref[d, :, n * WIDTH : (n + 1) * WIDTH] = scr[:, c : c + WIDTH]


def unpack_kernel(in_ref, dk_ref, dv_ref):
    for d in range(8):
        c = owner_columns(d)
        dk_ref[:, c : c + WIDTH] = in_ref[d, :, :WIDTH].astype(jnp.float32)
        dv_ref[:, c : c + WIDTH] = in_ref[d, :, WIDTH:].astype(jnp.float32)


def rows_kernel(low_ref, q_ref, do_ref, other_ref, qr_ref, dor_ref):
    low = low_ref[0]
    for x, (src, dst) in enumerate(((q_ref, qr_ref), (do_ref, dor_ref))):
        for h in range(LOCAL_HEADS):
            for b in range(2):
                for n in range(2):
                    c = h * PAIR + n * BLOCK
                    rows = slice(b * BLOCK, (b + 1) * BLOCK)
                    here = pl.multiple_of((2 * low + b) * PAIR + n * BLOCK, BLOCK)
                    there = pl.multiple_of((2 * (1 - low) + b) * PAIR + n * BLOCK, BLOCK)
                    lane = pl.multiple_of(low * 2 * WIDTH + c, BLOCK)
                    dst[h, pl.ds(here, BLOCK), :] = src[rows, pl.ds(lane, BLOCK)]
                    dst[h, pl.ds(there, BLOCK), :] = other_ref[x, rows, c : c + BLOCK]


def columns_kernel(low_ref, mine_ref, other_ref, out_ref):
    low = low_ref[0]
    out_ref[:, pl.ds(pl.multiple_of(low * 2 * WIDTH, BLOCK), 2 * WIDTH)] = mine_ref[...]
    out_ref[:, pl.ds(pl.multiple_of((1 - low) * 2 * WIDTH, BLOCK), 2 * WIDTH)] = other_ref[...].astype(jnp.float32)


def visible(i, w):
    return i <= w <= i + BACK


def mask_of(hit_ref, start_ref, i, w):
    key_iota = lax.broadcasted_iota(jnp.int32, (BLOCK, BLOCK), 0)
    bound = start_ref[0:1, i * BLOCK : (i + 1) * BLOCK] - w * BLOCK
    if w < i + BACK:
        ok = key_iota >= jnp.where(hit_ref[i, w - i] > 0, -1, bound)
    else:
        ok = (key_iota >= bound) & (key_iota <= lax.broadcasted_iota(jnp.int32, (BLOCK, BLOCK), 1))
    return ok


def masked(ok, x):
    return jnp.concatenate(
        [jnp.where(ok, x[:, :BLOCK], NEG_LARGE), jnp.where(ok, x[:, BLOCK:], NEG_LARGE)], axis=1
    )


def fold(x, op):
    return op(x.reshape(BLOCK // 8, 8, PAIR), axis=0)


def stats_kernel(first_blocks, opening, closing, *refs):
    count = len(first_blocks)
    hit_ref, start_ref, q_ref, do_ref = refs[:4]
    pieces = refs[4 : 4 + count]
    rest = refs[4 + count :]
    if opening:
        state_in, rest = None, rest
    else:
        state_in, rest = rest[0], rest[1:]
    (out_ref,) = rest
    for h in range(LOCAL_HEADS):
        for i in range(Q_BLOCKS):
            lanes = slice(i * PAIR, (i + 1) * PAIR)
            qs = q_ref[h, lanes, :]
            dos = do_ref[h, lanes, :]
            if opening:
                top = jnp.full((8, PAIR), NEG_LARGE, jnp.float32)
                total = jnp.zeros((8, PAIR), jnp.float32)
                inner = jnp.zeros((8, PAIR), jnp.float32)
            else:
                top, total, inner = (state_in[h, n, :, lanes] for n in range(3))
            todo = []
            for ref, first in zip(pieces, first_blocks):
                seen = [w for w in (first, first + 1) if visible(i, w)]
                if seen:
                    todo.append((ref, seen, (seen[0] - first) * BLOCK))
            peak = top
            for ref, seen, row in todo:
                rows = slice(row, row + len(seen) * BLOCK)
                s = dot(ref[rows, h * HEAD_SIZE : (h + 1) * HEAD_SIZE], qs, 1, 1)
                dp = dot(ref[rows, WIDTH + h * HEAD_SIZE : WIDTH + (h + 1) * HEAD_SIZE], dos, 1, 1)
                for n, w in enumerate(seen):
                    part = slice(n * BLOCK, (n + 1) * BLOCK)
                    x = masked(mask_of(hit_ref, start_ref, i, w), s[part] * EXP2_SCALE)
                    higher = jnp.maximum(peak, fold(x, jnp.max))
                    weight = jnp.exp2(x.reshape(BLOCK // 8, 8, PAIR) - higher[None])
                    factor = jnp.exp2(peak - higher)
                    total = total * factor + jnp.sum(weight, axis=0)
                    inner = inner * factor + jnp.sum(weight * dp[part].reshape(BLOCK // 8, 8, PAIR), axis=0)
                    peak = higher
            if closing:
                top = jnp.max(peak, axis=0, keepdims=True)
                factor = jnp.exp2(peak - top)
                total = jnp.sum(total * factor, axis=0, keepdims=True)
                inner = jnp.sum(inner * factor, axis=0, keepdims=True)
                out_ref[h, 0:1, lanes] = top + jnp.log2(total)
                out_ref[h, 1:2, lanes] = inner / total
            else:
                out_ref[h, 0, :, lanes] = peak
                out_ref[h, 1, :, lanes] = total
                out_ref[h, 2, :, lanes] = inner


def stats(first_blocks, tables, pieces, state, closing):
    opening = state is None
    shape = f32(LOCAL_HEADS, 8, ROWS) if closing else f32(LOCAL_HEADS, 3, 8, ROWS)
    return call(
        functools.partial(stats_kernel, first_blocks, opening, closing),
        "stats",
        shape,
        [SMEM_SPEC] + [VMEM_SPEC] * (3 + len(pieces) + (not opening)),
    )(*tables, *pieces, *(() if opening else (state,)))


def grads_kernel(first_blocks, opening, closing, *refs):
    count = len(first_blocks)
    span = 2 * BLOCK
    query_blocks = min(Q_BLOCKS, first_blocks[-1] + 2)
    rows_used = query_blocks * PAIR
    if closing:
        low_ref, refs = refs[0], refs[1:]
    hit_ref, start_ref, q_ref, do_ref, norm_ref = refs[:5]
    pieces = refs[5 : 5 + count]
    rest = refs[5 + count :]
    if not opening:
        dqt_in, rest = rest[0], rest[1:]
    joined = first_blocks[-1] == BACK + 2
    if joined:
        out_refs, rest = [rest[0].at[n * span : (n + 1) * span] for n in range(count)], rest[1:]
    else:
        out_refs, rest = rest[:count], rest[count:]
    if closing:
        mine_ref, send_ref, p_scr, ds_scr, dq_scr = rest
    else:
        dqt_out, p_scr, ds_scr = rest
    for h in range(LOCAL_HEADS):
        kcols = slice(h * HEAD_SIZE, (h + 1) * HEAD_SIZE)
        vcols = slice(WIDTH + h * HEAD_SIZE, WIDTH + (h + 1) * HEAD_SIZE)
        for i in range(query_blocks):
            lanes = slice(i * PAIR, (i + 1) * PAIR)
            qs = q_ref[h, lanes, :]
            dos = do_ref[h, lanes, :]
            norm = norm_ref[h, 0:1, lanes]
            delta = norm_ref[h, 1:2, lanes]
            for m, (ref, first) in enumerate(zip(pieces, first_blocks)):
                seen = [w for w in (first, first + 1) if visible(i, w)]
                for w in (first, first + 1):
                    if w not in seen and not joined:
                        at = slice(m * span + (w - first) * BLOCK, m * span + (w - first + 1) * BLOCK)
                        p_scr[h, at, lanes] = jnp.zeros((BLOCK, PAIR), jnp.bfloat16)
                        ds_scr[h, at, lanes] = jnp.zeros((BLOCK, PAIR), jnp.bfloat16)
                if not seen:
                    continue
                row = (seen[0] - first) * BLOCK
                rows = slice(row, row + len(seen) * BLOCK)
                s = dot(ref[rows, kcols], qs, 1, 1)
                dp = dot(ref[rows, vcols], dos, 1, 1)
                for n, w in enumerate(seen):
                    part = slice(n * BLOCK, (n + 1) * BLOCK)
                    x = masked(mask_of(hit_ref, start_ref, i, w), s[part] * EXP2_SCALE - norm)
                    prob = jnp.exp2(x)
                    at = slice(m * span + (w - first) * BLOCK, m * span + (w - first + 1) * BLOCK)
                    p_scr[h, at, lanes] = prob.astype(jnp.bfloat16)
                    ds_scr[h, at, lanes] = ((prob * SCORE_SCALE) * (dp[part] - delta)).astype(jnp.bfloat16)
        keys = [ref[:, kcols] for ref in pieces]
        keys = keys[0] if count == 1 else jnp.concatenate(keys, axis=0)
        used = slice(0, rows_used)
        if joined:
            dv, dk, dqt = [], [], []
            for r in range(Q_BLOCKS):
                rows, later = slice(r * BLOCK, (r + 1) * BLOCK), slice(r * PAIR, ROWS)
                dv.append(dot(p_scr[h, rows, later], do_ref[h, later, :], 1, 0))
                dk.append(dot(ds_scr[h, rows, later], q_ref[h, later, :], 1, 0))
                earlier, lanes = slice(0, (r + 1) * BLOCK), slice(r * PAIR, (r + 1) * PAIR)
                dqt.append(dot(keys[earlier], ds_scr[h, earlier, lanes], 0, 0))
            dv, dk = jnp.concatenate(dv, axis=0), jnp.concatenate(dk, axis=0)
            dqt = jnp.concatenate(dqt, axis=1)
        else:
            ds = ds_scr[h, :, used]
            dv = dot(p_scr[h, :, used], do_ref[h, used, :], 1, 0)
            dk = dot(ds, q_ref[h, used, :], 1, 0)
            dqt = dot(keys, ds, 0, 0)
        if not opening:
            dqt = dqt + dqt_in[h]
        for m, out in enumerate(out_refs):
            out[:, kcols] = dk[m * span : (m + 1) * span].astype(out.dtype)
            out[:, vcols] = dv[m * span : (m + 1) * span].astype(out.dtype)
        if closing:
            for b in range(2 * Q_BLOCKS):
                c = h * PAIR + (b % 2) * BLOCK
                dq_scr[b // 2 * BLOCK : (b // 2 + 1) * BLOCK, c : c + BLOCK] = dqt[:, b * BLOCK : (b + 1) * BLOCK].T
        else:
            dqt_out[h, :, used] = dqt
            if rows_used < ROWS:
                dqt_out[h, :, rows_used:] = jnp.zeros((HEAD_SIZE, ROWS - rows_used), jnp.float32)
    if closing:
        low = low_ref[0]
        mine_ref[...] = dq_scr[pl.ds(pl.multiple_of(low * SPAN, SPAN), SPAN), :]
        send_ref[...] = dq_scr[pl.ds(pl.multiple_of((1 - low) * SPAN, SPAN), SPAN), :].astype(jnp.bfloat16)


def grads(first_blocks, tables, norm, pieces, dqt, dtypes, low=None, light=False):
    opening, closing = dqt is None, low is not None
    count = len(pieces)
    rows = SPAN * count // len(dtypes)
    outs = [jax.ShapeDtypeStruct((rows, 2 * WIDTH), d) for d in dtypes]
    outs += [f32(SPAN, 2 * WIDTH), bf16(SPAN, 2 * WIDTH)] if closing else [f32(LOCAL_HEADS, HEAD_SIZE, ROWS)]
    scratch = [pltpu.VMEM((LOCAL_HEADS, SPAN * count, ROWS), jnp.bfloat16)] * 2
    if closing:
        scratch.append(pltpu.VMEM((SLAB, 2 * WIDTH), jnp.float32))
    operands = tables + (norm,) + tuple(pieces) + (() if opening else (dqt,))
    specs = [SMEM_SPEC] + [VMEM_SPEC] * (len(operands) - 1)
    if closing:
        operands, specs = (low,) + operands, [SMEM_SPEC] + specs
    aliases = {} if opening or closing else {len(operands) - 1: len(dtypes)}
    return call(
        functools.partial(grads_kernel, first_blocks, opening, closing),
        "grads",
        tuple(outs),
        specs,
        scratch=scratch,
        aliases=aliases,
        light=light,
    )(*operands)


def finish_kernel(hit_ref, start_ref, q_ref, do_ref, piece, state, norm_ref, far_ref, dqt_ref, p_scr, ds_scr):
    tables = (hit_ref, start_ref, q_ref, do_ref)
    stats_kernel((0,), False, True, *tables, piece, state, norm_ref)
    grads_kernel((0,), True, False, *tables, norm_ref, piece, far_ref, dqt_ref, p_scr, ds_scr)


def finish(tables, piece, state):
    return call(
        finish_kernel,
        "finish",
        (f32(LOCAL_HEADS, 8, ROWS), bf16(SPAN, 2 * WIDTH), f32(LOCAL_HEADS, HEAD_SIZE, ROWS)),
        [SMEM_SPEC] + [VMEM_SPEC] * 5,
        scratch=[pltpu.VMEM((LOCAL_HEADS, SPAN, 2 * PAIR), jnp.bfloat16)] * 2,
    )(*tables, piece, state)


def per_device(queries, output_gradient, key_states, value_inputs, turn_ids, listed):
    slab = lax.axis_index(SLAB_AXES)
    low = lax.axis_index("xl")
    group = lax.axis_index("xh")
    low_ref = low.reshape(1)

    kv = pl.pallas_call(
        pack_kernel,
        out_shape=bf16(8, SPAN // 4, 2 * WIDTH),
        in_specs=[pl.BlockSpec(memory_space=pl.ANY)] * 2,
        out_specs=VMEM_SPEC,
        scratch_shapes=[pltpu.VMEM((SPAN // 4, KEY_VALUE_HEADS * HEAD_SIZE), jnp.bfloat16)] * 2
        + [pltpu.SemaphoreType.DMA((2,))],
        cost_estimate=pl.CostEstimate(flops=1024, bytes_accessed=1 << 25, transcendentals=0),
        name="pack",
    )(key_states, value_inputs)
    own = lax.all_to_all(kv, MEMBER_AXES, 0, 0, tiled=True)
    b0 = own[4:].reshape(SPAN, 2 * WIDTH)
    a0 = own[:4].reshape(SPAN, 2 * WIDTH)

    b1 = slab_shift(b0, 1)
    a1 = slab_shift(a0, 1)
    b2 = slab_shift(b1, 1)
    a2 = slab_shift(a1, 1)
    send = jnp.stack(
        [lax.dynamic_slice_in_dim(x, (1 - low) * 2 * WIDTH, 2 * WIDTH, 1) for x in (queries, output_gradient)]
    )
    other = low_swap(send)
    q, do = call(
        rows_kernel, "rows", (bf16(LOCAL_HEADS, ROWS, HEAD_SIZE),) * 2, [SMEM_SPEC] + [VMEM_SPEC] * 3
    )(low_ref, queries, output_gradient, other)

    padded = jnp.concatenate([jnp.full((HALO,), -1, turn_ids.dtype), turn_ids])
    window_turns = lax.dynamic_slice_in_dim(padded, slab * SLAB, WINDOW, 0)
    start = jnp.sum((window_turns[None, :] < window_turns[HALO:, None]).astype(jnp.int32), axis=1)[None, :]
    table = lax.dynamic_index_in_dim(listed, group, 0, keepdims=False)
    table = lax.dynamic_slice_in_dim(table, slab * Q_BLOCKS, Q_BLOCKS, 0)[:, ::-1]
    key_block = slab * Q_BLOCKS - BACK + jnp.arange(Q_BLOCKS)[:, None] + jnp.arange(BACK)[None, :]
    hit = jnp.where(key_block >= 0, table, 0)
    tables = (hit, start, q, do)

    state = stats((14, 16, 10, 12), tables, (a0, b0, a1, b1), None, False)
    b2, state = lax.optimization_barrier((b2, state))
    b3 = slab_shift(b2, 1)
    a3 = slab_shift(a2, 1)
    state = stats((6, 8), tables, (a2, b2), state, False)
    b3, state = lax.optimization_barrier((b3, state))
    b4 = slab_shift(b3, 1)
    state = stats((2, 4), tables, (a3, b3), state, False)
    b4, state = lax.optimization_barrier((b4, state))
    norm, gb4, dqt = finish(tables, b4, state)

    low16, full = jnp.bfloat16, jnp.float32
    def to_owners(x):
        return lax.all_to_all(x.reshape(8, SPAN // 4, 2 * WIDTH), MEMBER_AXES, 0, 0, tiled=True)

    def summed(part, arrived):
        return (part + arrived.astype(full)).astype(low16)

    def summed(part, arrived):
        return (part + arrived.astype(full)).astype(low16)

    def after(arrived, value):
        return lax.optimization_barrier((arrived, value))[1]

    rb = slab_shift(gb4, -1)
    ga3, gb3, dqt = grads((2, 4), tables, norm, (a3, b3), dqt, (low16, full), light=True)
    ra = slab_shift(ga3, -1)
    ga2, gb2, dqt = grads((6, 8), tables, norm, (a2, b2), dqt, (full, full), light=True)
    dqt, rb = lax.optimization_barrier((dqt, rb))
    rb = slab_shift(summed(gb3, rb), -1)
    ra = summed(ga2, ra)
    dqt = after(ra, dqt)
    ra = slab_shift(ra, -1)
    g0, dqt = grads((14, 16), tables, norm, (a0, b0), dqt, (full,), light=True)
    dqt, rb = lax.optimization_barrier((dqt, rb))
    rb = slab_shift(summed(gb2, rb), -1)
    ga1, gb1, mine, send = grads((10, 12), tables, norm, (a1, b1), dqt, (full, full), low_ref)
    ra = slab_shift(summed(ga1, ra), -1)
    rb = slab_shift(summed(gb1, rb), -1)
    other = low_swap(send)
    other, rb = lax.optimization_barrier((other, rb))
    total = lax.dynamic_update_slice(jnp.zeros((SLAB, 2 * WIDTH), low16), summed(g0[:SPAN], ra), (0, 0))
    total, rb = lax.optimization_barrier((total, rb))
    total = to_owners(lax.dynamic_update_slice(total, summed(g0[SPAN:], rb), (SPAN, 0)))
    grad_keys, grad_values = call(
        unpack_kernel, "unpack", (f32(SPAN // 4, KEY_VALUE_HEADS * HEAD_SIZE),) * 2, [VMEM_SPEC]
    )(total)

    grad_queries = call(
        columns_kernel, "columns", f32(SPAN, 4 * WIDTH), [SMEM_SPEC] + [VMEM_SPEC] * 2
    )(low_ref, mine, other)
    return grad_queries, grad_keys, grad_values


def solution(mesh):
    fine = Mesh(mesh.devices.reshape(4, 8, 2, 2, 2), ("y", "z", "xl", "xh", "core"))
    pb, ka = ("y", "z", "xl"), ("xh", "core")
    in_specs = (P(pb, ka), P(pb, ka), P(pb + ka, None), P(pb + ka, None), P(), P())
    out_specs = (P(pb, ka), P(pb + ka, None), P(pb + ka, None))
    return jax.shard_map(per_device, mesh=fine, in_specs=in_specs, out_specs=out_specs, check_vma=False)
```

```python
import functools
import math

import jax
import jax.numpy as jnp
from jax import lax
from jax.experimental import pallas as pl
from jax.experimental.pallas import tpu as pltpu
from jax.sharding import Mesh
from jax.sharding import PartitionSpec as P

KEY_VALUE_HEADS = 16
HEAD_SIZE = 128
BLOCK = 128
BACK = 14
SPAN = 256
SLAB = 2 * SPAN
HALO = BACK * BLOCK
WINDOW = HALO + SLAB
LOCAL_HEADS = 2
WIDTH = LOCAL_HEADS * HEAD_SIZE
Q_BLOCKS = SLAB // BLOCK
PAIR = 2 * BLOCK
ROWS = Q_BLOCKS * PAIR

SCORE_SCALE = 1.0 / 12.0
EXP2_SCALE = SCORE_SCALE * math.log2(math.e)
NEG_LARGE = -1e30

SLAB_AXES = ("y", "z")
MEMBER_AXES = ("xl", "xh", "core")

VMEM_SPEC = pl.BlockSpec(memory_space=pltpu.VMEM)
SMEM_SPEC = pl.BlockSpec(memory_space=pltpu.SMEM)


def slab_shift(x, by):
    count = lax.axis_size(SLAB_AXES)
    return lax.ppermute(x, SLAB_AXES, [(i, i + by) for i in range(count) if 0 <= i + by < count])


def low_swap(x):
    return lax.ppermute(x, "xl", [(0, 1), (1, 0)])


def dot(a, b, da, db):
    return lax.dot_general(a, b, (((da,), (db,)), ((), ())), preferred_element_type=jnp.float32)


def call(kernel, name, out_shape, in_specs, scratch=(), aliases=None, light=False):
    outs = out_shape if isinstance(out_shape, (tuple, list)) else (out_shape,)
    size = sum(o.size * o.dtype.itemsize for o in outs)
    return pl.pallas_call(
        kernel,
        out_shape=out_shape,
        in_specs=in_specs,
        out_specs=jax.tree.map(lambda _: VMEM_SPEC, out_shape),
        scratch_shapes=scratch,
        input_output_aliases=aliases or {},
        compiler_params=pltpu.CompilerParams(vmem_limit_bytes=32 * 1024 * 1024),
        cost_estimate=pl.CostEstimate(flops=1024, bytes_accessed=1 if light else size, transcendentals=0),
        name=name,
    )


def f32(*shape):
    return jax.ShapeDtypeStruct(shape, jnp.float32)


def bf16(*shape):
    return jax.ShapeDtypeStruct(shape, jnp.bfloat16)


def owner_columns(d):
    return (d % 4 * 4 + d // 4 * 2) * HEAD_SIZE


def pack_kernel(k_ref, v_ref, out_ref, k_scr, v_scr, sems):
    copies = [pltpu.make_async_copy(k_ref, k_scr, sems.at[0]), pltpu.make_async_copy(v_ref, v_scr, sems.at[1])]
    for copy in copies:
        copy.start()
    for n, (copy, scr) in enumerate(zip(copies, (k_scr, v_scr))):
        copy.wait()
        for d in range(8):
            c = owner_columns(d)
            out_ref[d, :, n * WIDTH : (n + 1) * WIDTH] = scr[:, c : c + WIDTH]


def unpack_kernel(in_ref, dk_ref, dv_ref):
    for d in range(8):
        c = owner_columns(d)
        dk_ref[:, c : c + WIDTH] = in_ref[d, :, :WIDTH].astype(jnp.float32)
        dv_ref[:, c : c + WIDTH] = in_ref[d, :, WIDTH:].astype(jnp.float32)


def rows_kernel(low_ref, q_ref, do_ref, other_ref, qr_ref, dor_ref):
    low = low_ref[0]
    for x, (src, dst) in enumerate(((q_ref, qr_ref), (do_ref, dor_ref))):
        for h in range(LOCAL_HEADS):
            for b in range(2):
                for n in range(2):
                    c = h * PAIR + n * BLOCK
                    rows = slice(b * BLOCK, (b + 1) * BLOCK)
                    here = pl.multiple_of((2 * low + b) * PAIR + n * BLOCK, BLOCK)
                    there = pl.multiple_of((2 * (1 - low) + b) * PAIR + n * BLOCK, BLOCK)
                    lane = pl.multiple_of(low * 2 * WIDTH + c, BLOCK)
                    dst[h, pl.ds(here, BLOCK), :] = src[rows, pl.ds(lane, BLOCK)]
                    dst[h, pl.ds(there, BLOCK), :] = other_ref[x, rows, c : c + BLOCK]


def columns_kernel(low_ref, mine_ref, other_ref, out_ref):
    low = low_ref[0]
    out_ref[:, pl.ds(pl.multiple_of(low * 2 * WIDTH, BLOCK), 2 * WIDTH)] = mine_ref[...]
    out_ref[:, pl.ds(pl.multiple_of((1 - low) * 2 * WIDTH, BLOCK), 2 * WIDTH)] = other_ref[...].astype(jnp.float32)


def visible(i, w):
    return i <= w <= i + BACK


def mask_of(hit_ref, start_ref, i, w):
    key_iota = lax.broadcasted_iota(jnp.int32, (BLOCK, BLOCK), 0)
    bound = start_ref[0:1, i * BLOCK : (i + 1) * BLOCK] - w * BLOCK
    if w < i + BACK:
        ok = key_iota >= jnp.where(hit_ref[i, w - i] > 0, -1, bound)
    else:
        ok = (key_iota >= bound) & (key_iota <= lax.broadcasted_iota(jnp.int32, (BLOCK, BLOCK), 1))
    return ok


def masked(ok, x):
    return jnp.concatenate(
        [jnp.where(ok, x[:, :BLOCK], NEG_LARGE), jnp.where(ok, x[:, BLOCK:], NEG_LARGE)], axis=1
    )


def fold(x, op):
    return op(x.reshape(BLOCK // 8, 8, PAIR), axis=0)


def stats_kernel(first_blocks, opening, closing, *refs):
    count = len(first_blocks)
    hit_ref, start_ref, q_ref, do_ref = refs[:4]
    pieces = refs[4 : 4 + count]
    rest = refs[4 + count :]
    if opening:
        state_in, rest = None, rest
    else:
        state_in, rest = rest[0], rest[1:]
    (out_ref,) = rest
    for h in range(LOCAL_HEADS):
        for i in range(Q_BLOCKS):
            lanes = slice(i * PAIR, (i + 1) * PAIR)
            qs = q_ref[h, lanes, :]
            dos = do_ref[h, lanes, :]
            if opening:
                top = jnp.full((8, PAIR), NEG_LARGE, jnp.float32)
                total = jnp.zeros((8, PAIR), jnp.float32)
                inner = jnp.zeros((8, PAIR), jnp.float32)
            else:
                top, total, inner = (state_in[h, n, :, lanes] for n in range(3))
            todo = []
            for ref, first in zip(pieces, first_blocks):
                seen = [w for w in (first, first + 1) if visible(i, w)]
                if seen:
                    todo.append((ref, seen, (seen[0] - first) * BLOCK))
            peak = top
            for ref, seen, row in todo:
                rows = slice(row, row + len(seen) * BLOCK)
                s = dot(ref[rows, h * HEAD_SIZE : (h + 1) * HEAD_SIZE], qs, 1, 1)
                dp = dot(ref[rows, WIDTH + h * HEAD_SIZE : WIDTH + (h + 1) * HEAD_SIZE], dos, 1, 1)
                for n, w in enumerate(seen):
                    part = slice(n * BLOCK, (n + 1) * BLOCK)
                    x = masked(mask_of(hit_ref, start_ref, i, w), s[part] * EXP2_SCALE)
                    higher = jnp.maximum(peak, fold(x, jnp.max))
                    weight = jnp.exp2(x.reshape(BLOCK // 8, 8, PAIR) - higher[None])
                    factor = jnp.exp2(peak - higher)
                    total = total * factor + jnp.sum(weight, axis=0)
                    inner = inner * factor + jnp.sum(weight * dp[part].reshape(BLOCK // 8, 8, PAIR), axis=0)
                    peak = higher
            if closing:
                top = jnp.max(peak, axis=0, keepdims=True)
                factor = jnp.exp2(peak - top)
                total = jnp.sum(total * factor, axis=0, keepdims=True)
                inner = jnp.sum(inner * factor, axis=0, keepdims=True)
                out_ref[h, 0:1, lanes] = top + jnp.log2(total)
                out_ref[h, 1:2, lanes] = inner / total
            else:
                out_ref[h, 0, :, lanes] = peak
                out_ref[h, 1, :, lanes] = total
                out_ref[h, 2, :, lanes] = inner


def stats(first_blocks, tables, pieces, state, closing):
    opening = state is None
    shape = f32(LOCAL_HEADS, 8, ROWS) if closing else f32(LOCAL_HEADS, 3, 8, ROWS)
    return call(
        functools.partial(stats_kernel, first_blocks, opening, closing),
        "stats",
        shape,
        [SMEM_SPEC] + [VMEM_SPEC] * (3 + len(pieces) + (not opening)),
    )(*tables, *pieces, *(() if opening else (state,)))


def grads_kernel(first_blocks, opening, closing, *refs):
    count = len(first_blocks)
    span = 2 * BLOCK
    query_blocks = min(Q_BLOCKS, first_blocks[-1] + 2)
    rows_used = query_blocks * PAIR
    if closing:
        low_ref, refs = refs[0], refs[1:]
    hit_ref, start_ref, q_ref, do_ref, norm_ref = refs[:5]
    pieces = refs[5 : 5 + count]
    rest = refs[5 + count :]
    if not opening:
        dqt_in, rest = rest[0], rest[1:]
    joined = first_blocks[-1] == BACK + 2
    if joined:
        out_refs, rest = [rest[0].at[n * span : (n + 1) * span] for n in range(count)], rest[1:]
    else:
        out_refs, rest = rest[:count], rest[count:]
    if closing:
        mine_ref, send_ref, p_scr, ds_scr, dq_scr = rest
    else:
        dqt_out, p_scr, ds_scr = rest
    for h in range(LOCAL_HEADS):
        kcols = slice(h * HEAD_SIZE, (h + 1) * HEAD_SIZE)
        vcols = slice(WIDTH + h * HEAD_SIZE, WIDTH + (h + 1) * HEAD_SIZE)
        for i in range(query_blocks):
            lanes = slice(i * PAIR, (i + 1) * PAIR)
            qs = q_ref[h, lanes, :]
            dos = do_ref[h, lanes, :]
            norm = norm_ref[h, 0:1, lanes]
            delta = norm_ref[h, 1:2, lanes]
            for m, (ref, first) in enumerate(zip(pieces, first_blocks)):
                seen = [w for w in (first, first + 1) if visible(i, w)]
                for w in (first, first + 1):
                    if w not in seen and not joined:
                        at = slice(m * span + (w - first) * BLOCK, m * span + (w - first + 1) * BLOCK)
                        p_scr[h, at, lanes] = jnp.zeros((BLOCK, PAIR), jnp.bfloat16)
                        ds_scr[h, at, lanes] = jnp.zeros((BLOCK, PAIR), jnp.bfloat16)
                if not seen:
                    continue
                row = (seen[0] - first) * BLOCK
                rows = slice(row, row + len(seen) * BLOCK)
                s = dot(ref[rows, kcols], qs, 1, 1)
                dp = dot(ref[rows, vcols], dos, 1, 1)
                for n, w in enumerate(seen):
                    part = slice(n * BLOCK, (n + 1) * BLOCK)
                    x = masked(mask_of(hit_ref, start_ref, i, w), s[part] * EXP2_SCALE - norm)
                    prob = jnp.exp2(x)
                    at = slice(m * span + (w - first) * BLOCK, m * span + (w - first + 1) * BLOCK)
                    p_scr[h, at, lanes] = prob.astype(jnp.bfloat16)
                    ds_scr[h, at, lanes] = ((prob * SCORE_SCALE) * (dp[part] - delta)).astype(jnp.bfloat16)
        keys = [ref[:, kcols] for ref in pieces]
        keys = keys[0] if count == 1 else jnp.concatenate(keys, axis=0)
        used = slice(0, rows_used)
        if joined:
            dv, dk, dqt = [], [], []
            for r in range(Q_BLOCKS):
                rows, later = slice(r * BLOCK, (r + 1) * BLOCK), slice(r * PAIR, ROWS)
                dv.append(dot(p_scr[h, rows, later], do_ref[h, later, :], 1, 0))
                dk.append(dot(ds_scr[h, rows, later], q_ref[h, later, :], 1, 0))
                earlier, lanes = slice(0, (r + 1) * BLOCK), slice(r * PAIR, (r + 1) * PAIR)
                dqt.append(dot(keys[earlier], ds_scr[h, earlier, lanes], 0, 0))
            dv, dk = jnp.concatenate(dv, axis=0), jnp.concatenate(dk, axis=0)
            dqt = jnp.concatenate(dqt, axis=1)
        else:
            ds = ds_scr[h, :, used]
            dv = dot(p_scr[h, :, used], do_ref[h, used, :], 1, 0)
            dk = dot(ds, q_ref[h, used, :], 1, 0)
            dqt = dot(keys, ds, 0, 0)
        if not opening:
            dqt = dqt + dqt_in[h]
        for m, out in enumerate(out_refs):
            out[:, kcols] = dk[m * span : (m + 1) * span].astype(out.dtype)
            out[:, vcols] = dv[m * span : (m + 1) * span].astype(out.dtype)
        if closing:
            for b in range(2 * Q_BLOCKS):
                c = h * PAIR + (b % 2) * BLOCK
                dq_scr[b // 2 * BLOCK : (b // 2 + 1) * BLOCK, c : c + BLOCK] = dqt[:, b * BLOCK : (b + 1) * BLOCK].T
        else:
            dqt_out[h, :, used] = dqt
            if rows_used < ROWS:
                dqt_out[h, :, rows_used:] = jnp.zeros((HEAD_SIZE, ROWS - rows_used), jnp.float32)
    if closing:
        low = low_ref[0]
        mine_ref[...] = dq_scr[pl.ds(pl.multiple_of(low * SPAN, SPAN), SPAN), :]
        send_ref[...] = dq_scr[pl.ds(pl.multiple_of((1 - low) * SPAN, SPAN), SPAN), :].astype(jnp.bfloat16)


def grads(first_blocks, tables, norm, pieces, dqt, dtypes, low=None, light=False):
    opening, closing = dqt is None, low is not None
    count = len(pieces)
    rows = SPAN * count // len(dtypes)
    outs = [jax.ShapeDtypeStruct((rows, 2 * WIDTH), d) for d in dtypes]
    outs += [f32(SPAN, 2 * WIDTH), bf16(SPAN, 2 * WIDTH)] if closing else [f32(LOCAL_HEADS, HEAD_SIZE, ROWS)]
    scratch = [pltpu.VMEM((LOCAL_HEADS, SPAN * count, ROWS), jnp.bfloat16)] * 2
    if closing:
        scratch.append(pltpu.VMEM((SLAB, 2 * WIDTH), jnp.float32))
    operands = tables + (norm,) + tuple(pieces) + (() if opening else (dqt,))
    specs = [SMEM_SPEC] + [VMEM_SPEC] * (len(operands) - 1)
    if closing:
        operands, specs = (low,) + operands, [SMEM_SPEC] + specs
    aliases = {} if opening or closing else {len(operands) - 1: len(dtypes)}
    return call(
        functools.partial(grads_kernel, first_blocks, opening, closing),
        "grads",
        tuple(outs),
        specs,
        scratch=scratch,
        aliases=aliases,
        light=light,
    )(*operands)


def finish_kernel(hit_ref, start_ref, q_ref, do_ref, piece, state, norm_ref, far_ref, dqt_ref, p_scr, ds_scr):
    tables = (hit_ref, start_ref, q_ref, do_ref)
    stats_kernel((0,), False, True, *tables, piece, state, norm_ref)
    grads_kernel((0,), True, False, *tables, norm_ref, piece, far_ref, dqt_ref, p_scr, ds_scr)


def finish(tables, piece, state):
    return call(
        finish_kernel,
        "finish",
        (f32(LOCAL_HEADS, 8, ROWS), bf16(SPAN, 2 * WIDTH), f32(LOCAL_HEADS, HEAD_SIZE, ROWS)),
        [SMEM_SPEC] + [VMEM_SPEC] * 5,
        scratch=[pltpu.VMEM((LOCAL_HEADS, SPAN, 2 * PAIR), jnp.bfloat16)] * 2,
    )(*tables, piece, state)


def per_device(queries, output_gradient, key_states, value_inputs, turn_ids, listed):
    slab = lax.axis_index(SLAB_AXES)
    low = lax.axis_index("xl")
    group = lax.axis_index("xh")
    low_ref = low.reshape(1)

    kv = pl.pallas_call(
        pack_kernel,
        out_shape=bf16(8, SPAN // 4, 2 * WIDTH),
        in_specs=[pl.BlockSpec(memory_space=pl.ANY)] * 2,
        out_specs=VMEM_SPEC,
        scratch_shapes=[pltpu.VMEM((SPAN // 4, KEY_VALUE_HEADS * HEAD_SIZE), jnp.bfloat16)] * 2
        + [pltpu.SemaphoreType.DMA((2,))],
        name="pack",
    )(key_states, value_inputs)
    own = lax.all_to_all(kv, MEMBER_AXES, 0, 0, tiled=True)
    b0 = own[4:].reshape(SPAN, 2 * WIDTH)
    a0 = own[:4].reshape(SPAN, 2 * WIDTH)

    b1 = slab_shift(b0, 1)
    a1 = slab_shift(a0, 1)
    b2 = slab_shift(b1, 1)
    a2 = slab_shift(a1, 1)
    send = jnp.stack(
        [lax.dynamic_slice_in_dim(x, (1 - low) * 2 * WIDTH, 2 * WIDTH, 1) for x in (queries, output_gradient)]
    )
    other = low_swap(send)
    q, do = call(
        rows_kernel, "rows", (bf16(LOCAL_HEADS, ROWS, HEAD_SIZE),) * 2, [SMEM_SPEC] + [VMEM_SPEC] * 3
    )(low_ref, queries, output_gradient, other)

    padded = jnp.concatenate([jnp.full((HALO,), -1, turn_ids.dtype), turn_ids])
    window_turns = lax.dynamic_slice_in_dim(padded, slab * SLAB, WINDOW, 0)
    start = jnp.sum((window_turns[None, :] < window_turns[HALO:, None]).astype(jnp.int32), axis=1)[None, :]
    table = lax.dynamic_index_in_dim(listed, group, 0, keepdims=False)
    table = lax.dynamic_slice_in_dim(table, slab * Q_BLOCKS, Q_BLOCKS, 0)[:, ::-1]
    key_block = slab * Q_BLOCKS - BACK + jnp.arange(Q_BLOCKS)[:, None] + jnp.arange(BACK)[None, :]
    hit = jnp.where(key_block >= 0, table, 0)
    tables = (hit, start, q, do)

    state = stats((14, 16, 10, 12), tables, (a0, b0, a1, b1), None, False)
    b2, state = lax.optimization_barrier((b2, state))
    b3 = slab_shift(b2, 1)
    a3 = slab_shift(a2, 1)
    state = stats((6, 8), tables, (a2, b2), state, False)
    b3, state = lax.optimization_barrier((b3, state))
    b4 = slab_shift(b3, 1)
    state = stats((2, 4), tables, (a3, b3), state, False)
    b4, state = lax.optimization_barrier((b4, state))
    norm, gb4, dqt = finish(tables, b4, state)

    low16, full = jnp.bfloat16, jnp.float32
    def to_owners(x):
        return lax.all_to_all(x.reshape(8, SPAN // 4, 2 * WIDTH), MEMBER_AXES, 0, 0, tiled=True)

    def summed(part, arrived):
        return (part + arrived.astype(full)).astype(low16)

    def summed(part, arrived):
        return (part + arrived.astype(full)).astype(low16)

    rb = slab_shift(gb4, -1)
    ga3, gb3, dqt = grads((2, 4), tables, norm, (a3, b3), dqt, (low16, full), light=True)
    ra = slab_shift(ga3, -1)
    g0, dqt = grads((14, 16), tables, norm, (a0, b0), dqt, (full,), light=True)
    dqt, rb = lax.optimization_barrier((dqt, rb))
    rb = slab_shift(summed(gb3, rb), -1)
    dqt, ra = lax.optimization_barrier((dqt, ra))
    ga2, gb2, dqt = grads((6, 8), tables, norm, (a2, b2), dqt, (full, full))
    ra = slab_shift(summed(ga2, ra), -1)
    dqt, rb = lax.optimization_barrier((dqt, rb))
    rb = slab_shift(summed(gb2, rb), -1)
    ga1, gb1, mine, send = grads((10, 12), tables, norm, (a1, b1), dqt, (full, full), low_ref)
    ra = slab_shift(summed(ga1, ra), -1)
    rb = slab_shift(summed(gb1, rb), -1)
    other = low_swap(send)
    other, rb = lax.optimization_barrier((other, rb))
    total = lax.dynamic_update_slice(jnp.zeros((SLAB, 2 * WIDTH), low16), summed(g0[:SPAN], ra), (0, 0))
    total, rb = lax.optimization_barrier((total, rb))
    total = to_owners(lax.dynamic_update_slice(total, summed(g0[SPAN:], rb), (SPAN, 0)))
    grad_keys, grad_values = call(
        unpack_kernel, "unpack", (f32(SPAN // 4, KEY_VALUE_HEADS * HEAD_SIZE),) * 2, [VMEM_SPEC]
    )(total)

    grad_queries = call(
        columns_kernel, "columns", f32(SPAN, 4 * WIDTH), [SMEM_SPEC] + [VMEM_SPEC] * 2
    )(low_ref, mine, other)
    return grad_queries, grad_keys, grad_values


def solution(mesh):
    fine = Mesh(mesh.devices.reshape(4, 8, 2, 2, 2), ("y", "z", "xl", "xh", "core"))
    pb, ka = ("y", "z", "xl"), ("xh", "core")
    in_specs = (P(pb, ka), P(pb, ka), P(pb + ka, None), P(pb + ka, None), P(), P())
    out_specs = (P(pb, ka), P(pb + ka, None), P(pb + ka, None))
    return jax.shard_map(per_device, mesh=fine, in_specs=in_specs, out_specs=out_specs, check_vma=False)
```

```python
import functools
import math

import jax
import jax.numpy as jnp
from jax import lax
from jax.experimental import pallas as pl
from jax.experimental.pallas import tpu as pltpu
from jax.sharding import Mesh
from jax.sharding import PartitionSpec as P

KEY_VALUE_HEADS = 16
HEAD_SIZE = 128
BLOCK = 128
BACK = 14
SPAN = 256
SLAB = 2 * SPAN
HALO = BACK * BLOCK
WINDOW = HALO + SLAB
LOCAL_HEADS = 2
WIDTH = LOCAL_HEADS * HEAD_SIZE
Q_BLOCKS = SLAB // BLOCK
PAIR = 2 * BLOCK
ROWS = Q_BLOCKS * PAIR

SCORE_SCALE = 1.0 / 12.0
EXP2_SCALE = SCORE_SCALE * math.log2(math.e)
NEG_LARGE = -1e30

SLAB_AXES = ("y", "z")
MEMBER_AXES = ("xl", "xh", "core")

VMEM_SPEC = pl.BlockSpec(memory_space=pltpu.VMEM)
SMEM_SPEC = pl.BlockSpec(memory_space=pltpu.SMEM)


def slab_shift(x, by):
    count = lax.axis_size(SLAB_AXES)
    return lax.ppermute(x, SLAB_AXES, [(i, i + by) for i in range(count) if 0 <= i + by < count])


def low_swap(x):
    return lax.ppermute(x, "xl", [(0, 1), (1, 0)])


def dot(a, b, da, db):
    return lax.dot_general(a, b, (((da,), (db,)), ((), ())), preferred_element_type=jnp.float32)


def call(kernel, name, out_shape, in_specs, scratch=(), aliases=None, light=False):
    outs = out_shape if isinstance(out_shape, (tuple, list)) else (out_shape,)
    size = sum(o.size * o.dtype.itemsize for o in outs)
    return pl.pallas_call(
        kernel,
        out_shape=out_shape,
        in_specs=in_specs,
        out_specs=jax.tree.map(lambda _: VMEM_SPEC, out_shape),
        scratch_shapes=scratch,
        input_output_aliases=aliases or {},
        compiler_params=pltpu.CompilerParams(vmem_limit_bytes=32 * 1024 * 1024),
        cost_estimate=pl.CostEstimate(flops=1024, bytes_accessed=1 if light else size, transcendentals=0),
        name=name,
    )


def f32(*shape):
    return jax.ShapeDtypeStruct(shape, jnp.float32)


def bf16(*shape):
    return jax.ShapeDtypeStruct(shape, jnp.bfloat16)


def owner_columns(d):
    return (d % 4 * 4 + d // 4 * 2) * HEAD_SIZE


def pack_kernel(k_ref, v_ref, out_ref, k_scr, v_scr, sems):
    copies = [pltpu.make_async_copy(k_ref, k_scr, sems.at[0]), pltpu.make_async_copy(v_ref, v_scr, sems.at[1])]
    for copy in copies:
        copy.start()
    for n, (copy, scr) in enumerate(zip(copies, (k_scr, v_scr))):
        copy.wait()
        for d in range(8):
            c = owner_columns(d)
            out_ref[d, :, n * WIDTH : (n + 1) * WIDTH] = scr[:, c : c + WIDTH]


def unpack_kernel(in_ref, dk_ref, dv_ref):
    for d in range(8):
        c = owner_columns(d)
        dk_ref[:, c : c + WIDTH] = in_ref[d, :, :WIDTH].astype(jnp.float32)
        dv_ref[:, c : c + WIDTH] = in_ref[d, :, WIDTH:].astype(jnp.float32)


def rows_kernel(low_ref, q_ref, do_ref, other_ref, qr_ref, dor_ref):
    low = low_ref[0]
    for x, (src, dst) in enumerate(((q_ref, qr_ref), (do_ref, dor_ref))):
        for h in range(LOCAL_HEADS):
            for b in range(2):
                for n in range(2):
                    c = h * PAIR + n * BLOCK
                    rows = slice(b * BLOCK, (b + 1) * BLOCK)
                    here = pl.multiple_of((2 * low + b) * PAIR + n * BLOCK, BLOCK)
                    there = pl.multiple_of((2 * (1 - low) + b) * PAIR + n * BLOCK, BLOCK)
                    lane = pl.multiple_of(low * 2 * WIDTH + c, BLOCK)
                    dst[h, pl.ds(here, BLOCK), :] = src[rows, pl.ds(lane, BLOCK)]
                    dst[h, pl.ds(there, BLOCK), :] = other_ref[x, rows, c : c + BLOCK]


def columns_kernel(low_ref, mine_ref, other_ref, out_ref):
    low = low_ref[0]
    out_ref[:, pl.ds(pl.multiple_of(low * 2 * WIDTH, BLOCK), 2 * WIDTH)] = mine_ref[...]
    out_ref[:, pl.ds(pl.multiple_of((1 - low) * 2 * WIDTH, BLOCK), 2 * WIDTH)] = other_ref[...].astype(jnp.float32)


def visible(i, w):
    return i <= w <= i + BACK


def mask_of(hit_ref, start_ref, i, w):
    key_iota = lax.broadcasted_iota(jnp.int32, (BLOCK, BLOCK), 0)
    bound = start_ref[0:1, i * BLOCK : (i + 1) * BLOCK] - w * BLOCK
    if w < i + BACK:
        ok = key_iota >= jnp.where(hit_ref[i, w - i] > 0, -1, bound)
    else:
        ok = (key_iota >= bound) & (key_iota <= lax.broadcasted_iota(jnp.int32, (BLOCK, BLOCK), 1))
    return ok


def masked(ok, x):
    return jnp.concatenate(
        [jnp.where(ok, x[:, :BLOCK], NEG_LARGE), jnp.where(ok, x[:, BLOCK:], NEG_LARGE)], axis=1
    )


def fold(x, op):
    return op(x.reshape(BLOCK // 8, 8, PAIR), axis=0)


def stats_kernel(first_blocks, opening, closing, *refs):
    count = len(first_blocks)
    hit_ref, start_ref, q_ref, do_ref = refs[:4]
    pieces = refs[4 : 4 + count]
    rest = refs[4 + count :]
    if opening:
        state_in, rest = None, rest
    else:
        state_in, rest = rest[0], rest[1:]
    (out_ref,) = rest
    for h in range(LOCAL_HEADS):
        for i in range(Q_BLOCKS):
            lanes = slice(i * PAIR, (i + 1) * PAIR)
            qs = q_ref[h, lanes, :]
            dos = do_ref[h, lanes, :]
            if opening:
                top = jnp.full((8, PAIR), NEG_LARGE, jnp.float32)
                total = jnp.zeros((8, PAIR), jnp.float32)
                inner = jnp.zeros((8, PAIR), jnp.float32)
            else:
                top, total, inner = (state_in[h, n, :, lanes] for n in range(3))
            todo = []
            for ref, first in zip(pieces, first_blocks):
                seen = [w for w in (first, first + 1) if visible(i, w)]
                if seen:
                    todo.append((ref, seen, (seen[0] - first) * BLOCK))
            peak = top
            for ref, seen, row in todo:
                rows = slice(row, row + len(seen) * BLOCK)
                s = dot(ref[rows, h * HEAD_SIZE : (h + 1) * HEAD_SIZE], qs, 1, 1)
                dp = dot(ref[rows, WIDTH + h * HEAD_SIZE : WIDTH + (h + 1) * HEAD_SIZE], dos, 1, 1)
                for n, w in enumerate(seen):
                    part = slice(n * BLOCK, (n + 1) * BLOCK)
                    x = masked(mask_of(hit_ref, start_ref, i, w), s[part] * EXP2_SCALE)
                    higher = jnp.maximum(peak, fold(x, jnp.max))
                    weight = jnp.exp2(x.reshape(BLOCK // 8, 8, PAIR) - higher[None])
                    factor = jnp.exp2(peak - higher)
                    total = total * factor + jnp.sum(weight, axis=0)
                    inner = inner * factor + jnp.sum(weight * dp[part].reshape(BLOCK // 8, 8, PAIR), axis=0)
                    peak = higher
            if closing:
                top = jnp.max(peak, axis=0, keepdims=True)
                factor = jnp.exp2(peak - top)
                total = jnp.sum(total * factor, axis=0, keepdims=True)
                inner = jnp.sum(inner * factor, axis=0, keepdims=True)
                out_ref[h, 0:1, lanes] = top + jnp.log2(total)
                out_ref[h, 1:2, lanes] = inner / total
            else:
                out_ref[h, 0, :, lanes] = peak
                out_ref[h, 1, :, lanes] = total
                out_ref[h, 2, :, lanes] = inner


def stats(first_blocks, tables, pieces, state, closing):
    opening = state is None
    shape = f32(LOCAL_HEADS, 8, ROWS) if closing else f32(LOCAL_HEADS, 3, 8, ROWS)
    return call(
        functools.partial(stats_kernel, first_blocks, opening, closing),
        "stats",
        shape,
        [SMEM_SPEC] + [VMEM_SPEC] * (3 + len(pieces) + (not opening)),
    )(*tables, *pieces, *(() if opening else (state,)))


def grads_kernel(first_blocks, opening, closing, *refs):
    count = len(first_blocks)
    span = 2 * BLOCK
    query_blocks = min(Q_BLOCKS, first_blocks[-1] + 2)
    rows_used = query_blocks * PAIR
    if closing:
        low_ref, refs = refs[0], refs[1:]
    hit_ref, start_ref, q_ref, do_ref, norm_ref = refs[:5]
    pieces = refs[5 : 5 + count]
    rest = refs[5 + count :]
    if not opening:
        dqt_in, rest = rest[0], rest[1:]
    joined = first_blocks[-1] == BACK + 2
    if joined:
        out_refs, rest = [rest[0].at[n * span : (n + 1) * span] for n in range(count)], rest[1:]
    else:
        out_refs, rest = rest[:count], rest[count:]
    if closing:
        mine_ref, send_ref, p_scr, ds_scr, dq_scr = rest
    else:
        dqt_out, p_scr, ds_scr = rest
    for h in range(LOCAL_HEADS):
        kcols = slice(h * HEAD_SIZE, (h + 1) * HEAD_SIZE)
        vcols = slice(WIDTH + h * HEAD_SIZE, WIDTH + (h + 1) * HEAD_SIZE)
        for i in range(query_blocks):
            lanes = slice(i * PAIR, (i + 1) * PAIR)
            qs = q_ref[h, lanes, :]
            dos = do_ref[h, lanes, :]
            norm = norm_ref[h, 0:1, lanes]
            delta = norm_ref[h, 1:2, lanes]
            for m, (ref, first) in enumerate(zip(pieces, first_blocks)):
                seen = [w for w in (first, first + 1) if visible(i, w)]
                for w in (first, first + 1):
                    if w not in seen and not joined:
                        at = slice(m * span + (w - first) * BLOCK, m * span + (w - first + 1) * BLOCK)
                        p_scr[h, at, lanes] = jnp.zeros((BLOCK, PAIR), jnp.bfloat16)
                        ds_scr[h, at, lanes] = jnp.zeros((BLOCK, PAIR), jnp.bfloat16)
                if not seen:
                    continue
                row = (seen[0] - first) * BLOCK
                rows = slice(row, row + len(seen) * BLOCK)
                s = dot(ref[rows, kcols], qs, 1, 1)
                dp = dot(ref[rows, vcols], dos, 1, 1)
                for n, w in enumerate(seen):
                    part = slice(n * BLOCK, (n + 1) * BLOCK)
                    x = masked(mask_of(hit_ref, start_ref, i, w), s[part] * EXP2_SCALE - norm)
                    prob = jnp.exp2(x)
                    at = slice(m * span + (w - first) * BLOCK, m * span + (w - first + 1) * BLOCK)
                    p_scr[h, at, lanes] = prob.astype(jnp.bfloat16)
                    ds_scr[h, at, lanes] = ((prob * SCORE_SCALE) * (dp[part] - delta)).astype(jnp.bfloat16)
        keys = [ref[:, kcols] for ref in pieces]
        keys = keys[0] if count == 1 else jnp.concatenate(keys, axis=0)
        used = slice(0, rows_used)
        if joined:
            dv, dk, dqt = [], [], []
            for r in range(Q_BLOCKS):
                rows, later = slice(r * BLOCK, (r + 1) * BLOCK), slice(r * PAIR, ROWS)
                dv.append(dot(p_scr[h, rows, later], do_ref[h, later, :], 1, 0))
                dk.append(dot(ds_scr[h, rows, later], q_ref[h, later, :], 1, 0))
                earlier, lanes = slice(0, (r + 1) * BLOCK), slice(r * PAIR, (r + 1) * PAIR)
                dqt.append(dot(keys[earlier], ds_scr[h, earlier, lanes], 0, 0))
            dv, dk = jnp.concatenate(dv, axis=0), jnp.concatenate(dk, axis=0)
            dqt = jnp.concatenate(dqt, axis=1)
        else:
            ds = ds_scr[h, :, used]
            dv = dot(p_scr[h, :, used], do_ref[h, used, :], 1, 0)
            dk = dot(ds, q_ref[h, used, :], 1, 0)
            dqt = dot(keys, ds, 0, 0)
        if not opening:
            dqt = dqt + dqt_in[h]
        for m, out in enumerate(out_refs):
            out[:, kcols] = dk[m * span : (m + 1) * span].astype(out.dtype)
            out[:, vcols] = dv[m * span : (m + 1) * span].astype(out.dtype)
        if closing:
            for b in range(2 * Q_BLOCKS):
                c = h * PAIR + (b % 2) * BLOCK
                dq_scr[b // 2 * BLOCK : (b // 2 + 1) * BLOCK, c : c + BLOCK] = dqt[:, b * BLOCK : (b + 1) * BLOCK].T
        else:
            dqt_out[h, :, used] = dqt
            if rows_used < ROWS:
                dqt_out[h, :, rows_used:] = jnp.zeros((HEAD_SIZE, ROWS - rows_used), jnp.float32)
    if closing:
        low = low_ref[0]
        mine_ref[...] = dq_scr[pl.ds(pl.multiple_of(low * SPAN, SPAN), SPAN), :]
        send_ref[...] = dq_scr[pl.ds(pl.multiple_of((1 - low) * SPAN, SPAN), SPAN), :].astype(jnp.bfloat16)


def grads(first_blocks, tables, norm, pieces, dqt, dtypes, low=None, light=False):
    opening, closing = dqt is None, low is not None
    count = len(pieces)
    rows = SPAN * count // len(dtypes)
    outs = [jax.ShapeDtypeStruct((rows, 2 * WIDTH), d) for d in dtypes]
    outs += [f32(SPAN, 2 * WIDTH), bf16(SPAN, 2 * WIDTH)] if closing else [f32(LOCAL_HEADS, HEAD_SIZE, ROWS)]
    scratch = [pltpu.VMEM((LOCAL_HEADS, SPAN * count, ROWS), jnp.bfloat16)] * 2
    if closing:
        scratch.append(pltpu.VMEM((SLAB, 2 * WIDTH), jnp.float32))
    operands = tables + (norm,) + tuple(pieces) + (() if opening else (dqt,))
    specs = [SMEM_SPEC] + [VMEM_SPEC] * (len(operands) - 1)
    if closing:
        operands, specs = (low,) + operands, [SMEM_SPEC] + specs
    aliases = {} if opening or closing else {len(operands) - 1: len(dtypes)}
    return call(
        functools.partial(grads_kernel, first_blocks, opening, closing),
        "grads",
        tuple(outs),
        specs,
        scratch=scratch,
        aliases=aliases,
        light=light,
    )(*operands)


def finish_kernel(hit_ref, start_ref, q_ref, do_ref, piece, state, norm_ref, far_ref, dqt_ref, p_scr, ds_scr):
    tables = (hit_ref, start_ref, q_ref, do_ref)
    stats_kernel((0,), False, True, *tables, piece, state, norm_ref)
    grads_kernel((0,), True, False, *tables, norm_ref, piece, far_ref, dqt_ref, p_scr, ds_scr)


def finish(tables, piece, state):
    return call(
        finish_kernel,
        "finish",
        (f32(LOCAL_HEADS, 8, ROWS), bf16(SPAN, 2 * WIDTH), f32(LOCAL_HEADS, HEAD_SIZE, ROWS)),
        [SMEM_SPEC] + [VMEM_SPEC] * 5,
        scratch=[pltpu.VMEM((LOCAL_HEADS, SPAN, 2 * PAIR), jnp.bfloat16)] * 2,
    )(*tables, piece, state)


def per_device(queries, output_gradient, key_states, value_inputs, turn_ids, listed):
    slab = lax.axis_index(SLAB_AXES)
    low = lax.axis_index("xl")
    group = lax.axis_index("xh")
    low_ref = low.reshape(1)

    kv = pl.pallas_call(
        pack_kernel,
        out_shape=bf16(8, SPAN // 4, 2 * WIDTH),
        in_specs=[pl.BlockSpec(memory_space=pl.ANY)] * 2,
        out_specs=VMEM_SPEC,
        scratch_shapes=[pltpu.VMEM((SPAN // 4, KEY_VALUE_HEADS * HEAD_SIZE), jnp.bfloat16)] * 2
        + [pltpu.SemaphoreType.DMA((2,))],
        name="pack",
    )(key_states, value_inputs)
    own = lax.all_to_all(kv, MEMBER_AXES, 0, 0, tiled=True)
    b0 = own[4:].reshape(SPAN, 2 * WIDTH)
    a0 = own[:4].reshape(SPAN, 2 * WIDTH)

    b1 = slab_shift(b0, 1)
    a1 = slab_shift(a0, 1)
    b2 = slab_shift(b1, 1)
    a2 = slab_shift(a1, 1)
    send = jnp.stack(
        [lax.dynamic_slice_in_dim(x, (1 - low) * 2 * WIDTH, 2 * WIDTH, 1) for x in (queries, output_gradient)]
    )
    other = low_swap(send)
    q, do = call(
        rows_kernel, "rows", (bf16(LOCAL_HEADS, ROWS, HEAD_SIZE),) * 2, [SMEM_SPEC] + [VMEM_SPEC] * 3
    )(low_ref, queries, output_gradient, other)

    padded = jnp.concatenate([jnp.full((HALO,), -1, turn_ids.dtype), turn_ids])
    window_turns = lax.dynamic_slice_in_dim(padded, slab * SLAB, WINDOW, 0)
    start = jnp.sum((window_turns[None, :] < window_turns[HALO:, None]).astype(jnp.int32), axis=1)[None, :]
    table = lax.dynamic_index_in_dim(listed, group, 0, keepdims=False)
    table = lax.dynamic_slice_in_dim(table, slab * Q_BLOCKS, Q_BLOCKS, 0)[:, ::-1]
    key_block = slab * Q_BLOCKS - BACK + jnp.arange(Q_BLOCKS)[:, None] + jnp.arange(BACK)[None, :]
    hit = jnp.where(key_block >= 0, table, 0)
    tables = (hit, start, q, do)

    state = stats((14, 16, 10, 12), tables, (a0, b0, a1, b1), None, False)
    b2, state = lax.optimization_barrier((b2, state))
    b3 = slab_shift(b2, 1)
    a3 = slab_shift(a2, 1)
    state = stats((6, 8), tables, (a2, b2), state, False)
    b3, state = lax.optimization_barrier((b3, state))
    b4 = slab_shift(b3, 1)
    state = stats((2, 4), tables, (a3, b3), state, False)
    b4, state = lax.optimization_barrier((b4, state))
    norm, gb4, dqt = finish(tables, b4, state)

    low16, full = jnp.bfloat16, jnp.float32
    def to_owners(x):
        return lax.all_to_all(x.reshape(8, SPAN // 4, 2 * WIDTH), MEMBER_AXES, 0, 0, tiled=True)

    def summed(part, arrived):
        return (part + arrived.astype(full)).astype(low16)

    def summed(part, arrived):
        return (part + arrived.astype(full)).astype(low16)

    rb = slab_shift(gb4, -1)
    ga3, gb3, dqt = grads((2, 4), tables, norm, (a3, b3), dqt, (low16, full), light=True)
    ra = slab_shift(ga3, -1)
    g0, dqt = grads((14, 16), tables, norm, (a0, b0), dqt, (full,), light=True)
    dqt = lax.optimization_barrier((rb, dqt))[1]
    rb = slab_shift(summed(gb3, rb), -1)
    dqt, ra = lax.optimization_barrier((dqt, ra))
    ga2, gb2, dqt = grads((6, 8), tables, norm, (a2, b2), dqt, (full, full))
    ra = slab_shift(summed(ga2, ra), -1)
    dqt, rb = lax.optimization_barrier((dqt, rb))
    rb = slab_shift(summed(gb2, rb), -1)
    ga1, gb1, mine, send = grads((10, 12), tables, norm, (a1, b1), dqt, (full, full), low_ref)
    ra = slab_shift(summed(ga1, ra), -1)
    rb = slab_shift(summed(gb1, rb), -1)
    other = low_swap(send)
    other, rb = lax.optimization_barrier((other, rb))
    total = lax.dynamic_update_slice(jnp.zeros((SLAB, 2 * WIDTH), low16), summed(g0[:SPAN], ra), (0, 0))
    total, rb = lax.optimization_barrier((total, rb))
    total = to_owners(lax.dynamic_update_slice(total, summed(g0[SPAN:], rb), (SPAN, 0)))
    grad_keys, grad_values = call(
        unpack_kernel, "unpack", (f32(SPAN // 4, KEY_VALUE_HEADS * HEAD_SIZE),) * 2, [VMEM_SPEC]
    )(total)

    grad_queries = call(
        columns_kernel, "columns", f32(SPAN, 4 * WIDTH), [SMEM_SPEC] + [VMEM_SPEC] * 2
    )(low_ref, mine, other)
    return grad_queries, grad_keys, grad_values


def solution(mesh):
    fine = Mesh(mesh.devices.reshape(4, 8, 2, 2, 2), ("y", "z", "xl", "xh", "core"))
    pb, ka = ("y", "z", "xl"), ("xh", "core")
    in_specs = (P(pb, ka), P(pb, ka), P(pb + ka, None), P(pb + ka, None), P(), P())
    out_specs = (P(pb, ka), P(pb + ka, None), P(pb + ka, None))
    return jax.shard_map(per_device, mesh=fine, in_specs=in_specs, out_specs=out_specs, check_vma=False)
```
